128 devices in a mesh: grp: 4 (over z_hi, core), seq: 32 (over z_lo, y, x).
Axes of the slice: x: 4, y: 4, z: 4 (z_hi: 2, z_lo: 2; z = z_hi * 2 + z_lo), core: 2. Of those that a mesh axis runs over, the one named last changes fastest.
Arguments:
- query: bfloat16 [4, 4096, 4096], P('grp', 'seq'), may hold values from -10 to 10
- key: bfloat16 [4, 4096, 4096], P('grp', 'seq'), may hold values from -10 to 10
- value: bfloat16 [4, 4096, 4096], P('grp', 'seq'), may hold values from -24 to 24
- gain_query: float32 [4096], replicated, may hold values from 0.1 to 1.9
- gain_key: float32 [4096], replicated, may hold values from 0.1 to 1.9
- ctrl_query: bfloat16 [4, 1024, 4096], P('grp', 'seq'), may hold values from -10 to 10
- ctrl_key: bfloat16 [4, 1024, 4096], P('grp', 'seq'), may hold values from -10 to 10
- ctrl_value: bfloat16 [4, 1024, 4096], P('grp', 'seq'), may hold values from -24 to 24
- ctrl_gain_query: float32 [4096], replicated, may hold values from 0.1 to 1.9
- ctrl_gain_key: float32 [4096], replicated, may hold values from 0.1 to 1.9
- gate_table: float32 [16, 4096], replicated, may hold values from 2 to 16
- levels: int32 [4, 8], P('grp'), may hold values from 0 to 15
- frame_map: int32 [4, 4096], P('grp', 'seq'), may hold values from 0 to 7, never falling along the last dimension, each value on 1 to 1024 neighbouring positions
- control_match: int32 [4, 1024], P('grp', 'seq'), may hold values from 0 to 4095, as said below
Outputs:
- mixed: bfloat16 [4, 4096, 4096], P('grp', 'seq')
The draws below stay inside these ranges and needn't reach their ends.
Inputs may be any that keep to these rules, and one draw needn't show every extreme that they name: `control_match`: the 1024 entries of one video are distinct.
All inputs are finite; a program needn't handle non-finite values.
Results may differ from the reference program's by a relative error of at most 0.0055.
The reference program's roundings to bfloat16 on the way count: a program that leaves them out, or rounds other values in their place, can miss the bound.
Values may be sent and summed in bfloat16 or wider, within the bound.
No kernel may reach another device: no remote copies, remote signals or barrier semaphores. Data moves between devices by JAX's collectives and lax.ppermute only.
A program may use at most 64 MiB of HBM per device.

```python
import math
import jax
import jax.numpy as jnp
import numpy as np
from jax import lax

HEADS = 32
HEAD_DIM = 128
WIDTH = 4096
FRAMES = 8
LEVELS = 16
VIDEOS = 4
SEQ_LEN = 4096
CTRL_LEN = 1024


def draw_query(key, part):
    key = jax.random.fold_in(key, 1)
    return jnp.clip(jax.random.normal(key, (VIDEOS, SEQ_LEN, WIDTH)), -6.0, 6.0).astype(jnp.bfloat16)


def draw_key(key, part):
    key = jax.random.fold_in(key, 2)
    return jnp.clip(jax.random.normal(key, (VIDEOS, SEQ_LEN, WIDTH)), -6.0, 6.0).astype(jnp.bfloat16)


def draw_ctrl_query(key, part):
    key = jax.random.fold_in(key, 3)
    return jnp.clip(jax.random.normal(key, (VIDEOS, CTRL_LEN, WIDTH)), -6.0, 6.0).astype(jnp.bfloat16)


def draw_ctrl_key(key, part):
    key = jax.random.fold_in(key, 4)
    return jnp.clip(jax.random.normal(key, (VIDEOS, CTRL_LEN, WIDTH)), -6.0, 6.0).astype(jnp.bfloat16)


def draw_control_match(key, part):
    key = jax.random.fold_in(key, 5)
    video_keys = jax.random.split(key, VIDEOS)

    def one_video(video_key):
        k_inner, k_order = jax.random.split(video_key)
        inner = jax.random.permutation(k_inner, SEQ_LEN - 2)[:CTRL_LEN - 2] + 1
        ends = jnp.array([0, SEQ_LEN - 1], dtype=jnp.int32)
        chosen = jnp.concatenate([inner.astype(jnp.int32), ends])
        return jax.random.permutation(k_order, chosen).astype(jnp.int32)
    return jax.vmap(one_video)(video_keys)


def place_ends(values, key, low, high):
    shape = values.shape
    spot = [jax.random.randint(jax.random.fold_in(key, axis), (), 0, shape[axis]) for axis in range(len(shape))]
    values = values.at[tuple(spot)].set(low)
    longest = shape.index(max(shape))
    spot[longest] = (spot[longest] + 1) % shape[longest]
    return values.at[tuple(spot)].set(high)


def block_scale(stream_key, dims, cuts, smallest, high):
    level, own = 1.0, jax.random.fold_in(stream_key, 6)
    for axis_at, shards_of in cuts:
        heights = jnp.exp(jax.random.uniform(jax.random.fold_in(own, axis_at), (shards_of,), jnp.float32, smallest / len(cuts), high / len(cuts)))
        level = level * jnp.repeat(heights, dims[axis_at] // shards_of).reshape([-1 if axis == axis_at else 1 for axis in range(len(dims))])
    return level


def profile(count, total, most, lean):
    weights = [(1 << 20) // math.isqrt(grade ** lean) + 1 for grade in range(2, count + 1)]
    spare, given = total - most - (count - 1), [1] * (count - 1)
    while spare > 0:
        movable = [i for i in range(count - 1) if given[i] < most]
        pool, left = sum([weights[i] for i in movable]), spare
        for i in movable:
            more = min(most - given[i], max(1, left * weights[i] // pool), spare)
            given[i] = given[i] + more
            spare = spare - more
    return np.array([most] + given)


def uneven_parts(own_key, count, total, reach, lean):
    if count == 2:
        one = jax.random.randint(own_key, (), max(1, total - reach), min(reach, total - 1) + 1)
        return jnp.stack([one, total - one])
    lengths = jnp.asarray(profile(count, total, reach, lean), jnp.int32)
    couples = (count - 1) // 2
    giver, receiver = lengths[1:1 + 2 * couples:2], lengths[2:2 + 2 * couples:2]
    margin = jnp.minimum(giver - 1, reach - receiver)
    passed = jax.random.randint(jax.random.fold_in(own_key, 1), (couples,), 0, 1 << 20) % (margin + 1)
    lengths = lengths.at[1:1 + 2 * couples:2].set(giver - passed).at[2:2 + 2 * couples:2].set(receiver + passed)
    return lengths[jax.random.permutation(jax.random.fold_in(own_key, 2), count)]


def normal_values(rng, dims, deviation, bound, pieces=(), kind=jnp.bfloat16):
    values = deviation * jax.random.normal(rng, dims, jnp.float32)
    if pieces:
        values = values * block_scale(rng, dims, pieces, -0.22, 0.18)
    return jnp.clip(values, -bound, bound).astype(kind)


def setup_inputs(seed: int = 0) -> dict:
    key_list = jax.random.split(jax.random.key(seed), 15)
    query = draw_query(jax.random.fold_in(key_list[14], 71), 0)
    key = draw_key(jax.random.fold_in(key_list[14], 71), 0)
    value = normal_values(key_list[2], (VIDEOS, SEQ_LEN, WIDTH), 4.0, 24.0, ((0, 4), (1, 32)))
    gain_query = jnp.clip(1.0 + 0.18 * jax.random.normal(key_list[3], (WIDTH,), jnp.float32), 0.1, 1.9)
    gain_key = jnp.clip(1.0 + 0.18 * jax.random.normal(key_list[4], (WIDTH,), jnp.float32), 0.1, 1.9)
    ctrl_query = draw_ctrl_query(jax.random.fold_in(key_list[14], 71), 0)
    ctrl_key = draw_ctrl_key(jax.random.fold_in(key_list[14], 71), 0)
    ctrl_value = normal_values(key_list[7], (VIDEOS, CTRL_LEN, WIDTH), 4.0, 24.0, ((0, 4), (1, 32)))
    ctrl_gain_query = jnp.clip(1.0 + 0.18 * jax.random.normal(key_list[8], (WIDTH,), jnp.float32), 0.1, 1.9)
    ctrl_gain_key = jnp.clip(1.0 + 0.18 * jax.random.normal(key_list[9], (WIDTH,), jnp.float32), 0.1, 1.9)
    gate_table = jnp.clip(jnp.exp(jax.random.uniform(key_list[10], (LEVELS, WIDTH), jnp.float32, math.log(2.0), math.log(16.0))), 2.0, 16.0)
    levels = place_ends(jax.random.randint(key_list[11], (VIDEOS, FRAMES), 0, LEVELS), jax.random.fold_in(key_list[11], 1), 0, LEVELS - 1).astype(jnp.int32)
    frame_map = jax.vmap(lambda own: jnp.searchsorted(jnp.cumsum(uneven_parts(own, FRAMES, SEQ_LEN, 2 * SEQ_LEN // FRAMES, 1)), jnp.arange(SEQ_LEN), side="right"))(jax.random.split(key_list[12], VIDEOS)).reshape((VIDEOS, SEQ_LEN)).astype(jnp.int32)
    control_match = draw_control_match(jax.random.fold_in(key_list[14], 71), 0)
    return {"query": query, "key": key, "value": value, "gain_query": gain_query, "gain_key": gain_key, "ctrl_query": ctrl_query, "ctrl_key": ctrl_key, "ctrl_value": ctrl_value, "ctrl_gain_query": ctrl_gain_query, "ctrl_gain_key": ctrl_gain_key, "gate_table": gate_table, "levels": levels, "frame_map": frame_map, "control_match": control_match}


def rms_round(values, gain):
    wide = values.astype(jnp.float32)
    mean_sq = lax.optimization_barrier(jnp.mean(wide * wide, axis=-1, keepdims=True))
    return (wide * lax.rsqrt(mean_sq + 1e-06) * gain).astype(jnp.bfloat16)

def attend_head(queries, keys, values, query_frames, key_frames, causal):
    rows = queries.shape[0]
    block = min(512, rows)
    factor = 1.0 / math.sqrt(keys.shape[1])
    q_blocks = queries.reshape(rows // block, block, queries.shape[1])
    if causal:
        f_blocks = query_frames.reshape(rows // block, block)
    else:
        f_blocks = jnp.zeros((rows // block, block), jnp.int32)

    def one_block(pair):
        part, frames = pair
        scores = jnp.dot(part, keys.T, preferred_element_type=jnp.float32) * factor
        if causal:
            scores = jnp.where(key_frames[None, :] <= frames[:, None], scores, -1e+30)
        top = lax.optimization_barrier(jnp.max(scores, axis=1, keepdims=True))
        expo = jnp.exp(scores - top)
        weights = (expo / lax.optimization_barrier(jnp.sum(expo, axis=1, keepdims=True))).astype(jnp.bfloat16)
        return jnp.dot(weights, values, preferred_element_type=jnp.float32).astype(jnp.bfloat16)
    result = lax.map(one_block, (q_blocks, f_blocks))
    return result.reshape(rows, values.shape[1])

def attend_heads(q_three, k_three, v_three, query_frames, key_frames, causal):
    q_first = jnp.moveaxis(q_three, 1, 0)
    k_first = jnp.moveaxis(k_three, 1, 0)
    v_first = jnp.moveaxis(v_three, 1, 0)

    def one_head(triple):
        return attend_head(triple[0], triple[1], triple[2], query_frames, key_frames, causal)
    result = lax.map(one_head, (q_first, k_first, v_first))
    return jnp.moveaxis(result, 0, 1)

def level_rows(frames, frame_levels):
    picks = frames[:, None] == jnp.arange(FRAMES, dtype=jnp.int32)[None, :]
    return lax.optimization_barrier(jnp.sum(jnp.where(picks, frame_levels[None, :], 0), axis=1)).astype(jnp.int32)

def gate_rows(frames, frame_levels, table):
    row_levels = level_rows(frames, frame_levels)
    onehot = (row_levels[:, None] == jnp.arange(LEVELS, dtype=jnp.int32)[None, :]).astype(jnp.float32)
    return jnp.dot(onehot, table, precision=lax.Precision.HIGHEST)

def reference(query, key, value, gain_query, gain_key, ctrl_query, ctrl_key, ctrl_value, ctrl_gain_query, ctrl_gain_key, gate_table, levels, frame_map, control_match):
    shape_main = (SEQ_LEN, HEADS, HEAD_DIM)
    shape_ctrl = (CTRL_LEN, HEADS, HEAD_DIM)
    hints = []
    for video in range(VIDEOS):
        cq = rms_round(ctrl_query[video], ctrl_gain_query).reshape(shape_ctrl)
        ck = rms_round(ctrl_key[video], ctrl_gain_key).reshape(shape_ctrl)
        cv = ctrl_value[video].reshape(shape_ctrl)
        hints.append(attend_heads(cq, ck, cv, None, None, False).reshape(CTRL_LEN, WIDTH))
    outputs = []
    for video in range(VIDEOS):
        qn = rms_round(query[video], gain_query).reshape(shape_main)
        kn = rms_round(key[video], gain_key).reshape(shape_main)
        vv = value[video].reshape(shape_main)
        frames = frame_map[video]
        attn = attend_heads(qn, kn, vv, frames, frames, True).reshape(SEQ_LEN, WIDTH)
        gate = gate_rows(frames, levels[video], gate_table)
        hint = hints[(video - 1) % VIDEOS]
        added = jnp.zeros((SEQ_LEN, WIDTH), jnp.float32).at[control_match[video]].add(hint.astype(jnp.float32))
        outputs.append((gate * attn.astype(jnp.float32) + added).astype(jnp.bfloat16))
    return jnp.stack(outputs)
```

```python
import math

import jax
import jax.numpy as jnp
from jax import lax
from jax.experimental import pallas as pl
from jax.experimental.pallas import tpu as pltpu
from jax.sharding import PartitionSpec as P

HEADS = 32
HEAD_DIM = 128
WIDTH = 4096
TOK_DEV = 128
CTRL_DEV = 32
FRAMES = 8
LEVELS = 16
SEQ = 4096
CTRL = 1024
META = 16
ROW_K = 0
ROW_V = TOK_DEV
ROW_M = 2 * TOK_DEV
ROW_C = ROW_M + META
ROWS = ROW_C + 3 * CTRL_DEV
SCALE = 1.0 / math.sqrt(HEAD_DIM)
SCALE2 = SCALE * math.log2(math.e)
QB = 512
KB = 512
VMEM_LIMIT = 56 * 1024 * 1024
F32 = jnp.float32
BF16 = jnp.bfloat16


def params():
    return pltpu.CompilerParams(vmem_limit_bytes=VMEM_LIMIT)


def rms_round(values, gain):
    wide = values.astype(F32)
    mean_sq = jnp.mean(wide * wide, axis=-1, keepdims=True)
    return (wide * lax.rsqrt(mean_sq + 1e-06) * gain).astype(BF16)


def lay_heads(out_ref, row, values):
    rows = values.shape[0]
    for head in range(HEADS):
        out_ref[head, row : row + rows, :] = values[:, head * HEAD_DIM : (head + 1) * HEAD_DIM]


def pack_kernel(k, v, cq, ck, cv, gk, gcq, gck, meta, out):
    step = 32
    for at in range(0, TOK_DEV, step):
        lay_heads(out, ROW_K + at, rms_round(k[at : at + step, :], gk[...]))
        lay_heads(out, ROW_V + at, v[at : at + step, :])
    lay_heads(out, ROW_C, rms_round(cq[...], gcq[...]))
    lay_heads(out, ROW_C + CTRL_DEV, rms_round(ck[...], gck[...]))
    lay_heads(out, ROW_C + 2 * CTRL_DEV, cv[...])
    for head in range(HEADS):
        out[head, ROW_M : ROW_M + META, :] = meta[...]


def pack_query_kernel(q, gq, out):
    step = 32
    for at in range(0, TOK_DEV, step):
        lay_heads(out, at, rms_round(q[at : at + step, :], gq[...]))


def ctrl_kernel(first, out, held, sem):
    copy = pltpu.make_async_copy(first.at[:, pl.ds(ROW_C, 3 * CTRL_DEV), :], held, sem)
    copy.start()
    copy.wait()
    keys = held[:, CTRL_DEV : 2 * CTRL_DEV, :].reshape(CTRL, HEAD_DIM)
    values = held[:, 2 * CTRL_DEV :, :].reshape(CTRL, HEAD_DIM)
    for part in range(4):
        queries = held[part * 8 : part * 8 + 8, :CTRL_DEV, :].reshape(256, HEAD_DIM)
        scores = lax.dot_general(queries, keys, (((1,), (1,)), ((), ())), preferred_element_type=F32)
        top = jnp.max(scores, axis=1, keepdims=True)
        expo = jnp.exp2((scores - top) * SCALE2)
        total = jnp.sum(expo, axis=1, keepdims=True)
        weights = (expo * (1.0 / total)).astype(BF16)
        out[part * 256 : part * 256 + 256, :] = jnp.dot(
            weights, values, preferred_element_type=F32
        ).astype(BF16)


def main_kernel(places, table, first, query, hint, out, kv, meta, k_t, v_one, acc, top_ref, sems):
    copies = [
        pltpu.make_async_copy(first.at[:, pl.ds(ROW_K, 2 * TOK_DEV), :], kv, sems.at[0]),
        pltpu.make_async_copy(first.at[:, pl.ds(ROW_M, META), :], meta, sems.at[1]),
    ]
    for copy in copies:
        copy.start()
    for copy in copies:
        copy.wait()
    wide_meta = meta[...].astype(F32)
    frames = wide_meta[:, 0, :]
    high = jnp.sum(wide_meta[:, 1, :].reshape(8, 4, 128), axis=1)
    low = jnp.sum(wide_meta[:, 2, :].reshape(8, 4, 128), axis=1)
    match = high * 64.0 + low
    ends = [
        jnp.sum(jnp.where(frames <= f + 0.5, 1.0, 0.0)).astype(jnp.int32) for f in range(FRAMES)
    ]

    def end_of(token):
        end = jnp.int32(SEQ)
        for f in reversed(range(FRAMES)):
            end = jnp.where(ends[f] > token, ends[f], end)
        return end

    for block in range(HEADS):
        k_t[:, block * 128 : block * 128 + 128] = (
            kv[block, :TOK_DEV, :].astype(F32).T.astype(BF16)
        )
        v_one[block * 128 : block * 128 + 128, :HEAD_DIM] = kv[block, TOK_DEV:, :]
    v_one[:, HEAD_DIM:] = jnp.ones((SEQ, HEAD_DIM), BF16)

    def one_block(i, carry):
        base = i * QB
        queries = query[pl.ds(i * (QB // TOK_DEV), QB // TOK_DEV), :, :].reshape(QB, HEAD_DIM)
        n_full = end_of(base) // KB
        n_all = (end_of(base + QB - 1) + KB - 1) // KB
        token = lax.broadcasted_iota(jnp.int32, (QB, 128), 0) + base
        limit = jnp.full((QB, 128), SEQ, jnp.int32)
        for f in reversed(range(FRAMES)):
            limit = jnp.where(ends[f] > token, ends[f], limit)
        acc[...] = jnp.zeros_like(acc)
        top_ref[...] = jnp.full_like(top_ref, -1e30)

        def step(j, masked):
            at = pl.multiple_of(j * KB, KB)
            scores = jnp.dot(queries, k_t[:, pl.ds(at, KB)], preferred_element_type=F32)
            if masked:
                column = lax.broadcasted_iota(jnp.int32, (QB, KB), 1) + at
                scores = jnp.where(column < limit[:, :1], scores, -1e30)
            old = top_ref[...]
            new = jnp.maximum(old, jnp.max(scores, axis=1, keepdims=True))
            top_ref[...] = new
            expo = jnp.exp2((scores - new[:, :1]) * SCALE2).astype(BF16)
            part = jnp.dot(expo, v_one[pl.ds(at, KB), :], preferred_element_type=F32)
            back = jnp.exp2((old - new) * SCALE2)
            acc[:, :HEAD_DIM] = acc[:, :HEAD_DIM] * back + part[:, :HEAD_DIM]
            acc[:, HEAD_DIM:] = acc[:, HEAD_DIM:] * back + part[:, HEAD_DIM:]

        @pl.loop(0, n_full)
        def _(j):
            step(j, False)

        @pl.loop(n_full, n_all)
        def _(j):
            step(j, True)

        attn = (acc[:, :HEAD_DIM] / acc[:, HEAD_DIM:]).astype(BF16).astype(F32)
        gate = jnp.broadcast_to(table[pl.ds(places[1], 1), :], (QB, HEAD_DIM))
        for f in range(1, FRAMES):
            gate = jnp.where(token >= ends[f - 1], table[pl.ds(places[1 + f], 1), :], gate)
        spot = token.astype(F32)
        picks = jnp.concatenate(
            [jnp.where(spot == match[g : g + 1, :], 1.0, 0.0).astype(BF16) for g in range(8)], axis=1
        )
        added = jnp.dot(picks, hint[...], preferred_element_type=F32)
        mixed = (gate * attn + added).astype(BF16)
        out[pl.ds(i * (QB // TOK_DEV), QB // TOK_DEV), :, :] = mixed.reshape(
            QB // TOK_DEV, TOK_DEV, HEAD_DIM
        )
        return carry

    lax.fori_loop(0, SEQ // QB, one_block, 0)


def whole():
    return pl.BlockSpec(memory_space=pltpu.VMEM)


def exchange(block):
    return lax.all_to_all(block, "seq", split_axis=0, concat_axis=0, tiled=True)


def body(
    query,
    key,
    value,
    gain_query,
    gain_key,
    ctrl_query,
    ctrl_key,
    ctrl_value,
    ctrl_gain_query,
    ctrl_gain_key,
    gate_table,
    levels,
    frame_map,
    control_match,
):
    here = lax.axis_index("seq")
    lane = jnp.arange(128, dtype=jnp.int32)
    spread = jnp.where(lane // CTRL_DEV == here % 4, jnp.tile(control_match[0], 4), 0)
    meta = jnp.concatenate(
        [
            frame_map,
            (spread // 64)[None],
            (spread % 64)[None],
            jnp.zeros((META - 3, 128), jnp.int32),
        ],
        axis=0,
    ).astype(BF16)
    packed = pl.pallas_call(
        pack_kernel,
        out_shape=jax.ShapeDtypeStruct((HEADS, ROWS, HEAD_DIM), BF16),
        in_specs=[whole()] * 9,
        out_specs=whole(),
        compiler_params=params(),
        cost_estimate=pl.CostEstimate(flops=8_000_000, bytes_accessed=6_000_000, transcendentals=0),
        name="pack",
    )(
        key[0],
        value[0],
        ctrl_query[0],
        ctrl_key[0],
        ctrl_value[0],
        gain_key[None],
        ctrl_gain_query[None],
        ctrl_gain_key[None],
        meta,
    )
    first = exchange(packed)
    packed_query = pl.pallas_call(
        pack_query_kernel,
        out_shape=jax.ShapeDtypeStruct((HEADS, TOK_DEV, HEAD_DIM), BF16),
        in_specs=[whole()] * 2,
        out_specs=whole(),
        compiler_params=params(),
        cost_estimate=pl.CostEstimate(flops=4_000_000, bytes_accessed=2_000_000, transcendentals=0),
        name="pack_query",
    )(query[0], gain_query[None])
    second = exchange(packed_query)
    hint = pl.pallas_call(
        ctrl_kernel,
        out_shape=jax.ShapeDtypeStruct((CTRL, HEAD_DIM), BF16),
        in_specs=[pl.BlockSpec(memory_space=pl.ANY)],
        out_specs=whole(),
        scratch_shapes=[
            pltpu.VMEM((HEADS, 3 * CTRL_DEV, HEAD_DIM), BF16),
            pltpu.SemaphoreType.DMA,
        ],
        compiler_params=params(),
        cost_estimate=pl.CostEstimate(
            flops=4 * CTRL * CTRL * HEAD_DIM, bytes_accessed=1_000_000, transcendentals=CTRL * CTRL
        ),
        name="ctrl_attention",
    )(first)
    groups = lax.axis_size("grp")
    hint = lax.ppermute(hint, "grp", [((i - 1) % groups, i) for i in range(groups)])
    places = jnp.concatenate([here[None].astype(jnp.int32), levels[0]])
    mixed = pl.pallas_call(
        main_kernel,
        grid_spec=pltpu.PrefetchScalarGridSpec(
            num_scalar_prefetch=1,
            grid=(1,),
            in_specs=[
                pl.BlockSpec((LEVELS, HEAD_DIM), lambda i, places: (0, places[0])),
                pl.BlockSpec(memory_space=pl.ANY),
                whole(),
                whole(),
            ],
            out_specs=whole(),
            scratch_shapes=[
                pltpu.VMEM((HEADS, 2 * TOK_DEV, HEAD_DIM), BF16),
                pltpu.VMEM((HEADS, META, HEAD_DIM), BF16),
                pltpu.VMEM((HEAD_DIM, SEQ), BF16),
                pltpu.VMEM((SEQ, 2 * HEAD_DIM), BF16),
                pltpu.VMEM((QB, 2 * HEAD_DIM), F32),
                pltpu.VMEM((QB, HEAD_DIM), F32),
                pltpu.SemaphoreType.DMA((2,)),
            ],
        ),
        out_shape=jax.ShapeDtypeStruct((HEADS, TOK_DEV, HEAD_DIM), BF16),
        compiler_params=params(),
        cost_estimate=pl.CostEstimate(
            flops=4 * SEQ * SEQ * HEAD_DIM, bytes_accessed=5_000_000, transcendentals=SEQ * SEQ
        ),
        name="main_attention",
    )(places, gate_table, first, second, hint)
    back = exchange(mixed)
    return jnp.swapaxes(back, 0, 1).reshape(1, TOK_DEV, WIDTH)


def solution(mesh):
    return jax.shard_map(
        body,
        mesh=mesh,
        in_specs=(
            P("grp", "seq", None),
            P("grp", "seq", None),
            P("grp", "seq", None),
            P(),
            P(),
            P("grp", "seq", None),
            P("grp", "seq", None),
            P("grp", "seq", None),
            P(),
            P(),
            P(),
            P("grp", None),
            P("grp", "seq"),
            P("grp", "seq"),
        ),
        out_specs=P("grp", "seq", None),
        check_vma=False,
    )
```

```python
import math

import jax
import jax.numpy as jnp
from jax import lax
from jax.experimental import pallas as pl
from jax.experimental.pallas import tpu as pltpu
from jax.sharding import PartitionSpec as P

HEADS = 32
HEAD_DIM = 128
WIDTH = 4096
TOK_DEV = 128
CTRL_DEV = 32
FRAMES = 8
LEVELS = 16
SEQ = 4096
CTRL = 1024
META = 16
ROW_M = 3 * CTRL_DEV
ROWS_C = ROW_M + META
ROWS = 3 * TOK_DEV
SCALE2 = math.log2(math.e) / math.sqrt(HEAD_DIM)
QB = 512
KB = 1024
VR = HEAD_DIM + 16
SAFE = 2.0**100
VMEM_LIMIT = 20 * 1024 * 1024
F32 = jnp.float32
BF16 = jnp.bfloat16


def params():
    return pltpu.CompilerParams(vmem_limit_bytes=VMEM_LIMIT)


def whole():
    return pl.BlockSpec(memory_space=pltpu.VMEM)


def rms_round(values, gain):
    wide = values.astype(F32)
    mean_sq = jnp.mean(wide * wide, axis=-1, keepdims=True)
    return (wide * lax.rsqrt(mean_sq + 1e-06) * gain).astype(BF16)


def lay_heads(out_ref, row, values):
    rows = values.shape[0]
    for head in range(HEADS):
        out_ref[head, row : row + rows, :] = values[:, head * HEAD_DIM : (head + 1) * HEAD_DIM]


def pack_ctrl_kernel(cq, ck, cv, gcq, gck, frames, match, out):
    lay_heads(out, 0, rms_round(cq[...], gcq[...]))
    lay_heads(out, CTRL_DEV, rms_round(ck[...], gck[...]))
    lay_heads(out, 2 * CTRL_DEV, cv[...])
    spots = jnp.concatenate([match[...]] * 4, axis=1)
    row = lax.broadcasted_iota(jnp.int32, (META, 128), 0)
    meta = jnp.where(row == 0, frames[...], jnp.where(row == 1, spots // 64, spots % 64))
    meta = jnp.where(row < 3, meta, 0).astype(F32).astype(BF16)
    for head in range(HEADS):
        out[head, ROW_M:, :] = meta


def pack_main_kernel(q, k, v, gq, gk, out):
    step = 32
    for at in range(0, TOK_DEV, step):
        lay_heads(out, at, rms_round(q[at : at + step, :], gq[...]))
        lay_heads(out, TOK_DEV + at, rms_round(k[at : at + step, :], gk[...]))
        lay_heads(out, 2 * TOK_DEV + at, v[at : at + step, :])


def ctrl_kernel(first, hint, ends):
    frames = first[:, ROW_M:, :].astype(F32)[:, 0, :]
    for f in range(FRAMES):
        ends[f] = jnp.sum(jnp.where(frames <= f + 0.5, 1.0, 0.0)).astype(jnp.int32)
    keys = first[:, CTRL_DEV : 2 * CTRL_DEV, :].reshape(CTRL, HEAD_DIM)
    values = first[:, 2 * CTRL_DEV : ROW_M, :].reshape(CTRL, HEAD_DIM)
    for part in range(4):
        queries = first[part * 8 : part * 8 + 8, :CTRL_DEV, :].reshape(256, HEAD_DIM)
        scores = lax.dot_general(queries, keys, (((1,), (1,)), ((), ())), preferred_element_type=F32)
        top = jnp.max(scores, axis=1, keepdims=True)
        expo = jnp.exp2((scores - top) * SCALE2)
        total = jnp.sum(expo, axis=1, keepdims=True)
        weights = (expo * (1.0 / total)).astype(BF16)
        hint[part * 256 : part * 256 + 256, :] = jnp.dot(
            weights, values, preferred_element_type=F32
        ).astype(BF16)


def place_kernel(places, table, first, hint, added, gates):
    for f in range(FRAMES):
        gates[f : f + 1, :] = table[pl.ds(places[1 + f], 1), :]
    meta = first[:, ROW_M:, :].astype(F32)
    spots = (meta[:, 1, :] * 64.0 + meta[:, 2, :]).reshape(8, 4, 128)
    source = lax.broadcasted_iota(jnp.int32, (8, 4, 128), 1)
    lane = lax.broadcasted_iota(jnp.int32, (8, 4, 128), 2)
    match = jnp.sum(jnp.where(lane // CTRL_DEV == source, spots, 0.0), axis=1)
    for i in range(SEQ // QB):
        spot = (lax.broadcasted_iota(jnp.int32, (QB, 128), 0) + i * QB).astype(F32)
        picks = jnp.concatenate(
            [jnp.where(spot == match[g : g + 1, :], 1.0, 0.0).astype(BF16) for g in range(8)], axis=1
        )
        rows = jnp.dot(picks, hint[...], preferred_element_type=F32).astype(BF16)
        added[i * (QB // TOK_DEV) : (i + 1) * (QB // TOK_DEV), :, :] = rows.reshape(
            QB // TOK_DEV, TOK_DEV, HEAD_DIM
        )


def main_kernel(ends_ref, gates, second, added, out, v_t, acc, sums, top_ref):
    ends = [ends_ref[f] for f in range(FRAMES)]

    def end_of(token):
        end = jnp.int32(SEQ)
        for f in reversed(range(FRAMES)):
            end = jnp.where(ends[f] > token, ends[f], end)
        return end

    for block in range(HEADS):
        v_t[:HEAD_DIM, block * 128 : block * 128 + 128] = (
            second[block, 2 * TOK_DEV :, :].astype(F32).T.astype(BF16)
        )
    v_t[HEAD_DIM:, :] = jnp.ones((VR - HEAD_DIM, SEQ), BF16)

    def limit_of(base):
        column = lax.broadcasted_iota(jnp.int32, (8, QB), 1) + base
        limit = jnp.full((8, QB), SEQ, jnp.int32)
        for f in reversed(range(FRAMES)):
            limit = jnp.where(ends[f] > column, ends[f], limit)
        return limit[:1, :]

    def scores_of(i, j, masked):
        queries = second[pl.ds(i * (QB // TOK_DEV), QB // TOK_DEV), :TOK_DEV, :]
        q_t = queries.reshape(QB, HEAD_DIM).astype(F32).T.astype(BF16)
        keys = second[pl.ds(j * (KB // TOK_DEV), KB // TOK_DEV), TOK_DEV : 2 * TOK_DEV, :]
        scores = jnp.dot(keys.reshape(KB, HEAD_DIM), q_t, preferred_element_type=F32)
        return scores

    def visible(limit, j):
        return lax.broadcasted_iota(jnp.int32, (KB, QB), 0) < limit - j * KB

    def values_of(j):
        return v_t[:, pl.ds(pl.multiple_of(j * KB, KB), KB)]

    def finish(i, total):
        base = i * QB
        token = lax.broadcasted_iota(jnp.int32, (QB, HEAD_DIM), 0) + base
        attn = (total[:HEAD_DIM, :] / total[HEAD_DIM : HEAD_DIM + 1, :]).T.astype(BF16).astype(F32)
        gate = jnp.broadcast_to(gates[0:1, :], (QB, HEAD_DIM))
        for f in range(1, FRAMES):
            gate = jnp.where(token >= ends[f - 1], gates[f : f + 1, :], gate)
        at = pl.ds(i * (QB // TOK_DEV), QB // TOK_DEV)
        rows = added[at, :, :].reshape(QB, HEAD_DIM).astype(F32)
        out[at, :, :] = (gate * attn + rows).astype(BF16).reshape(QB // TOK_DEV, TOK_DEV, HEAD_DIM)

    def quick_block(i, carry):
        base = i * QB
        n_full = end_of(base) // KB
        n_all = (end_of(base + QB - 1) + KB - 1) // KB
        limit = limit_of(base)
        queries = second[pl.ds(i * (QB // TOK_DEV), QB // TOK_DEV), :TOK_DEV, :]
        q_t = queries.reshape(QB, HEAD_DIM).astype(F32).T.astype(BF16)
        acc[...] = jnp.zeros_like(acc)

        def step(j, masked):
            keys = second[pl.ds(j * (KB // TOK_DEV), KB // TOK_DEV), TOK_DEV : 2 * TOK_DEV, :]
            scores = jnp.dot(keys.reshape(KB, HEAD_DIM), q_t, preferred_element_type=F32)
            expo = jnp.exp2(scores * SCALE2)
            if masked:
                expo = jnp.where(visible(limit, j), expo, 0.0)
            acc[...] += jnp.dot(values_of(j), expo.astype(BF16), preferred_element_type=F32)

        @pl.loop(0, n_full)
        def _(j):
            step(j, False)

        @pl.loop(n_full, n_all)
        def _(j):
            step(j, True)

        sums[pl.ds(i, 1), :] = acc[HEAD_DIM : HEAD_DIM + 1, :]
        finish(i, acc)
        return carry

    def full_block(i, carry):
        base = i * QB
        n_all = (end_of(base + QB - 1) + KB - 1) // KB
        limit = limit_of(base)
        acc[...] = jnp.zeros_like(acc)
        top_ref[...] = jnp.full_like(top_ref, -1e30)

        @pl.loop(0, n_all)
        def _(j):
            scores = jnp.where(visible(limit, j), scores_of(i, j, True), -1e30)
            old = top_ref[:1, :]
            new = jnp.maximum(old, jnp.max(scores, axis=0, keepdims=True))
            expo = jnp.exp2((scores - new) * SCALE2).astype(BF16)
            part = jnp.dot(values_of(j), expo, preferred_element_type=F32)
            acc[...] = acc[...] * jnp.exp2((old - new) * SCALE2) + part
            top_ref[...] = jnp.broadcast_to(new, top_ref.shape)

        finish(i, acc)
        return carry

    lax.fori_loop(0, SEQ // QB, quick_block, 0)
    good = (sums[...] > 1.0 / SAFE) & (sums[...] < SAFE)
    count = jnp.sum(jnp.where(good, 1.0, 0.0))

    @pl.when(count < SEQ - 0.5)
    def _():
        lax.fori_loop(0, SEQ // QB, full_block, 0)


def unpack_kernel(rows, out):
    for head in range(HEADS):
        out[:, head * HEAD_DIM : (head + 1) * HEAD_DIM] = rows[head, :, :]


def cost(flops, moved, transcendentals=0):
    return pl.CostEstimate(flops=flops, bytes_accessed=moved, transcendentals=transcendentals)


def shape(*dims, dtype=BF16):
    return jax.ShapeDtypeStruct(dims, dtype)


def run_main(ends, gates, second, added):
    return pl.pallas_call(
        main_kernel,
        out_shape=shape(HEADS, TOK_DEV, HEAD_DIM),
        in_specs=[pl.BlockSpec(memory_space=pltpu.SMEM), whole(), whole(), whole()],
        out_specs=whole(),
        scratch_shapes=[
            pltpu.VMEM((VR, SEQ), BF16),
            pltpu.VMEM((VR, QB), F32),
            pltpu.VMEM((SEQ // QB, QB), F32),
            pltpu.VMEM((8, QB), F32),
        ],
        compiler_params=params(),
        cost_estimate=cost(4 * SEQ * SEQ * HEAD_DIM, 5_000_000, SEQ * SEQ),
        name="main_attention",
    )(ends, gates, second, added)


def exchange(block):
    return lax.all_to_all(block, "seq", split_axis=0, concat_axis=0, tiled=True)


def body(
    query,
    key,
    value,
    gain_query,
    gain_key,
    ctrl_query,
    ctrl_key,
    ctrl_value,
    ctrl_gain_query,
    ctrl_gain_key,
    gate_table,
    levels,
    frame_map,
    control_match,
):
    packed = pl.pallas_call(
        pack_ctrl_kernel,
        out_shape=shape(HEADS, ROWS_C, HEAD_DIM),
        in_specs=[whole()] * 7,
        out_specs=whole(),
        compiler_params=params(),
        cost_estimate=cost(2_000_000, 2_000_000),
        name="pack_ctrl",
    )(
        ctrl_query[0],
        ctrl_key[0],
        ctrl_value[0],
        ctrl_gain_query[None],
        ctrl_gain_key[None],
        frame_map,
        control_match,
    )
    first = exchange(packed)
    packed_main = pl.pallas_call(
        pack_main_kernel,
        out_shape=shape(HEADS, ROWS, HEAD_DIM),
        in_specs=[whole()] * 5,
        out_specs=whole(),
        compiler_params=params(),
        cost_estimate=cost(8_000_000, 6_000_000),
        name="pack_main",
    )(query[0], key[0], value[0], gain_query[None], gain_key[None])
    second = exchange(packed_main)
    hint, ends = pl.pallas_call(
        ctrl_kernel,
        out_shape=(shape(CTRL, HEAD_DIM), shape(FRAMES, dtype=jnp.int32)),
        in_specs=[whole()],
        out_specs=(whole(), pl.BlockSpec(memory_space=pltpu.SMEM)),
        compiler_params=params(),
        cost_estimate=cost(4 * CTRL * CTRL * HEAD_DIM, 1_000_000, CTRL * CTRL),
        name="ctrl_attention",
    )(first)
    groups = lax.axis_size("grp")
    hint = lax.ppermute(hint, "grp", [((i - 1) % groups, i) for i in range(groups)])
    places = jnp.concatenate([lax.axis_index("seq")[None].astype(jnp.int32), levels[0]])
    added, gates = pl.pallas_call(
        place_kernel,
        grid_spec=pltpu.PrefetchScalarGridSpec(
            num_scalar_prefetch=1,
            grid=(1,),
            in_specs=[
                pl.BlockSpec((LEVELS, HEAD_DIM), lambda i, places: (0, places[0])),
                whole(),
                whole(),
            ],
            out_specs=(whole(), whole()),
        ),
        out_shape=(shape(HEADS, TOK_DEV, HEAD_DIM), shape(FRAMES, HEAD_DIM, dtype=F32)),
        compiler_params=params(),
        cost_estimate=cost(2 * SEQ * CTRL * HEAD_DIM, 2_000_000),
        name="place_hints",
    )(places, gate_table, first, hint)
    mixed = run_main(ends, gates, second, added)
    back = exchange(mixed)
    return pl.pallas_call(
        unpack_kernel,
        out_shape=shape(TOK_DEV, WIDTH),
        in_specs=[whole()],
        out_specs=whole(),
        compiler_params=params(),
        cost_estimate=cost(0, 2_000_000),
        name="unpack",
    )(back)[None]


def solution(mesh):
    return jax.shard_map(
        body,
        mesh=mesh,
        in_specs=(
            P("grp", "seq", None),
            P("grp", "seq", None),
            P("grp", "seq", None),
            P(),
            P(),
            P("grp", "seq", None),
            P("grp", "seq", None),
            P("grp", "seq", None),
            P(),
            P(),
            P(),
            P("grp", None),
            P("grp", "seq"),
            P("grp", "seq"),
        ),
        out_specs=P("grp", "seq", None),
        check_vma=False,
    )
```

```python
import functools
import math

import jax
import jax.numpy as jnp
from jax import lax
from jax.experimental import pallas as pl
from jax.experimental.pallas import tpu as pltpu
from jax.sharding import PartitionSpec as P

HEADS = 32
HEAD_DIM = 128
WIDTH = 4096
TOK_DEV = 128
CTRL_DEV = 32
FRAMES = 8
LEVELS = 16
SEQ = 4096
CTRL = 1024
META = 16
ROW_M = 3 * CTRL_DEV
ROWS_C = ROW_M + META
ROWS = 3 * TOK_DEV
SCALE2 = math.log2(math.e) / math.sqrt(HEAD_DIM)
QB = 512
KB = 1024
PART = 512
WIDE = 8
VR = HEAD_DIM + 16
SAFE = 2.0**100
MIB = 1024 * 1024
F32 = jnp.float32
BF16 = jnp.bfloat16


def params(mib=20):
    return pltpu.CompilerParams(vmem_limit_bytes=mib * MIB)


def whole():
    return pl.BlockSpec(memory_space=pltpu.VMEM)


def rms_round(values, gain):
    wide = values.astype(F32)
    mean_sq = jnp.mean(wide * wide, axis=-1, keepdims=True)
    return (wide * lax.rsqrt(mean_sq + 1e-06) * gain).astype(BF16)


def lay_heads(out_ref, row, values):
    rows = values.shape[0]
    for head in range(HEADS):
        out_ref[head, row : row + rows, :] = values[:, head * HEAD_DIM : (head + 1) * HEAD_DIM]


def pack_ctrl_kernel(cq, ck, cv, gcq, gck, frames, match, out):
    lay_heads(out, 0, rms_round(cq[...], gcq[...]))
    lay_heads(out, CTRL_DEV, rms_round(ck[...], gck[...]))
    lay_heads(out, 2 * CTRL_DEV, cv[...])
    spots = jnp.concatenate([match[...]] * 4, axis=1)
    row = lax.broadcasted_iota(jnp.int32, (META, 128), 0)
    meta = jnp.where(row == 0, frames[...], jnp.where(row == 1, spots // 64, spots % 64))
    meta = jnp.where(row < 3, meta, 0).astype(F32).astype(BF16)
    for head in range(HEADS):
        out[head, ROW_M:, :] = meta


def pack_main_kernel(q, k, v, gq, gk, out):
    step = 32
    for at in range(0, TOK_DEV, step):
        lay_heads(out, at, rms_round(q[at : at + step, :], gq[...]))
        lay_heads(out, TOK_DEV + at, rms_round(k[at : at + step, :], gk[...]))
        lay_heads(out, 2 * TOK_DEV + at, v[at : at + step, :])


def ctrl_kernel(places, table, first, hint, ends, notes):
    meta = first[:, ROW_M:, :].astype(F32)
    frames = meta[:, 0, :]
    for f in range(FRAMES):
        ends[f] = jnp.sum(jnp.where(frames <= f + 0.5, 1.0, 0.0)).astype(jnp.int32)
        notes[8 + f : 9 + f, :] = table[pl.ds(places[1 + f], 1), :]
    spots = (meta[:, 1, :] * 64.0 + meta[:, 2, :]).reshape(8, 4, 128)
    source = lax.broadcasted_iota(jnp.int32, (8, 4, 128), 1)
    lane = lax.broadcasted_iota(jnp.int32, (8, 4, 128), 2)
    notes[:8, :] = jnp.sum(jnp.where(lane // CTRL_DEV == source, spots, 0.0), axis=1)
    keys = first[:, CTRL_DEV : 2 * CTRL_DEV, :].reshape(CTRL, HEAD_DIM)
    values = first[:, 2 * CTRL_DEV : ROW_M, :].reshape(CTRL, HEAD_DIM)
    for part in range(4):
        queries = first[part * 8 : part * 8 + 8, :CTRL_DEV, :].reshape(256, HEAD_DIM)
        scores = lax.dot_general(queries, keys, (((1,), (1,)), ((), ())), preferred_element_type=F32)
        top = jnp.max(scores, axis=1, keepdims=True)
        expo = jnp.exp2((scores - top) * SCALE2)
        total = jnp.sum(expo, axis=1, keepdims=True)
        weights = (expo * (1.0 / total)).astype(BF16)
        hint[part * 256 : part * 256 + 256, :] = jnp.dot(
            weights, values, preferred_element_type=F32
        ).astype(BF16)


def main_kernel(
    ends_ref, second, hint, notes_hbm, out, notes, match, gates, v_t, hint_t, acc, sums, top_ref, sem
):
    copy = pltpu.make_async_copy(notes_hbm, notes, sem)
    copy.start()
    ends = [ends_ref[f] for f in range(FRAMES)]

    def end_of(token):
        end = jnp.int32(SEQ)
        for f in reversed(range(FRAMES)):
            end = jnp.where(ends[f] > token, ends[f], end)
        return end

    for block in range(HEADS):
        v_t[:HEAD_DIM, block * 128 : block * 128 + 128] = (
            second[block, 2 * TOK_DEV :, :].astype(F32).T.astype(BF16)
        )
    v_t[HEAD_DIM:, :] = jnp.ones((VR - HEAD_DIM, SEQ), BF16)
    for g in range(CTRL // 128):
        hint_t[:, g * 128 : g * 128 + 128] = (
            hint[g * 128 : g * 128 + 128, :].astype(F32).T.astype(BF16)
        )

    copy.wait()
    for g in range(8):
        match[g * 128 : g * 128 + 128, :] = jnp.broadcast_to(notes[g : g + 1, :], (128, 128)).T
        gates[g, :, :] = jnp.broadcast_to(notes[8 + g : 9 + g, :], (128, 128)).T

    def limit_of(base):
        column = lax.broadcasted_iota(jnp.int32, (8, QB), 1) + base
        limit = jnp.full((8, QB), SEQ, jnp.int32)
        for f in reversed(range(FRAMES)):
            limit = jnp.where(ends[f] > column, ends[f], limit)
        return limit[:1, :]

    def scores_of(i, j, masked):
        queries = second[pl.ds(i * (QB // TOK_DEV), QB // TOK_DEV), :TOK_DEV, :]
        q_t = queries.reshape(QB, HEAD_DIM).astype(F32).T.astype(BF16)
        keys = second[pl.ds(j * (KB // TOK_DEV), KB // TOK_DEV), TOK_DEV : 2 * TOK_DEV, :]
        scores = jnp.dot(keys.reshape(KB, HEAD_DIM), q_t, preferred_element_type=F32)
        return scores

    def visible(limit, j):
        return lax.broadcasted_iota(jnp.int32, (KB, QB), 0) < limit - j * KB

    def values_of(j):
        return v_t[:, pl.ds(pl.multiple_of(j * KB, KB), KB)]

    def finish(i, total):
        base = i * QB
        attn = (total[:HEAD_DIM, :] / total[HEAD_DIM : HEAD_DIM + 1, :]).astype(BF16).astype(F32)
        picks, gate = [], []
        for at in range(0, QB, 128):
            spot = lax.broadcasted_iota(jnp.int32, (CTRL, 128), 1).astype(F32)
            shift = jnp.asarray(base + at, F32)
            picks.append(jnp.where(match[...] - shift == spot, 1.0, 0.0).astype(BF16))
            token = lax.broadcasted_iota(jnp.int32, (HEAD_DIM, 128), 1) + base + at
            level = gates[0]
            for f in range(1, FRAMES):
                level = jnp.where(token >= ends[f - 1], gates[f], level)
            gate.append(level)
        added = jnp.dot(hint_t[...], jnp.concatenate(picks, axis=1), preferred_element_type=F32)
        mixed = (jnp.concatenate(gate, axis=1) * attn + added).T.astype(BF16)
        rows = QB // TOK_DEV
        out[pl.ds(i * rows, rows), :, :] = mixed.reshape(rows, TOK_DEV, HEAD_DIM)

    def quick_block(i, carry):
        base = i * QB
        limit = limit_of(base)
        queries = second[pl.ds(i * (QB // TOK_DEV), QB // TOK_DEV), :TOK_DEV, :]
        q_t = queries.reshape(QB, HEAD_DIM).astype(F32).T.astype(BF16)

        def run(count):
            finish(jnp.maximum(i - 1, 0), acc)
            total = None
            edge = max(0, count - 3)
            cuts = list(range(0, edge, WIDE)) + list(range(edge, count)) + [count]
            for c, d in zip(cuts[:-1], cuts[1:]):
                per = PART // TOK_DEV
                keys = second[c * per : d * per, TOK_DEV : 2 * TOK_DEV, :]
                keys = keys.reshape((d - c) * PART, HEAD_DIM)
                expo = jnp.exp2(jnp.dot(keys, q_t, preferred_element_type=F32) * SCALE2)
                if c >= edge:
                    row = lax.broadcasted_iota(jnp.int32, expo.shape, 0)
                    expo = jnp.where(row < limit - c * PART, expo, 0.0)
                part = jnp.dot(
                    v_t[:, c * PART : d * PART], expo.astype(BF16), preferred_element_type=F32
                )
                total = part if total is None else total + part
            acc[...] = total

        parts = (end_of(base + QB - 1) + PART - 1) // PART
        for count in range(1, SEQ // PART + 1):
            pl.when(parts == count)(functools.partial(run, count))

        sums[pl.ds(i, 1), :] = acc[HEAD_DIM : HEAD_DIM + 1, :]
        return carry

    def full_block(i, carry):
        base = i * QB
        n_all = (end_of(base + QB - 1) + KB - 1) // KB
        limit = limit_of(base)
        acc[...] = jnp.zeros_like(acc)
        top_ref[...] = jnp.full_like(top_ref, -1e30)

        @pl.loop(0, n_all)
        def _(j):
            scores = jnp.where(visible(limit, j), scores_of(i, j, True), -1e30)
            old = top_ref[:1, :]
            new = jnp.maximum(old, jnp.max(scores, axis=0, keepdims=True))
            expo = jnp.exp2((scores - new) * SCALE2).astype(BF16)
            part = jnp.dot(values_of(j), expo, preferred_element_type=F32)
            acc[...] = acc[...] * jnp.exp2((old - new) * SCALE2) + part
            top_ref[...] = jnp.broadcast_to(new, top_ref.shape)

        finish(i, acc)
        return carry

    acc[...] = jnp.ones_like(acc)
    lax.fori_loop(0, SEQ // QB, quick_block, 0)
    finish(SEQ // QB - 1, acc)
    good = (sums[...] > 1.0 / SAFE) & (sums[...] < SAFE)
    count = jnp.sum(jnp.where(good, 1.0, 0.0))

    @pl.when(count < SEQ - 0.5)
    def _():
        lax.fori_loop(0, SEQ // QB, full_block, 0)


def unpack_kernel(rows, out):
    for head in range(HEADS):
        out[:, head * HEAD_DIM : (head + 1) * HEAD_DIM] = rows[head, :, :]


def cost(flops, moved, transcendentals=0):
    return pl.CostEstimate(flops=flops, bytes_accessed=moved, transcendentals=transcendentals)


def shape(*dims, dtype=BF16):
    return jax.ShapeDtypeStruct(dims, dtype)


def run_main(ends, second, hint, notes):
    return pl.pallas_call(
        main_kernel,
        out_shape=shape(HEADS, TOK_DEV, HEAD_DIM),
        in_specs=[pl.BlockSpec(memory_space=pltpu.SMEM)] + [whole()] * 2 + [pl.BlockSpec(memory_space=pltpu.HBM)],
        out_specs=whole(),
        scratch_shapes=[
            pltpu.VMEM((16, 128), F32),
            pltpu.VMEM((CTRL, 128), F32),
            pltpu.VMEM((FRAMES, HEAD_DIM, 128), F32),
            pltpu.VMEM((VR, SEQ), BF16),
            pltpu.VMEM((HEAD_DIM, CTRL), BF16),
            pltpu.VMEM((VR, QB), F32),
            pltpu.VMEM((SEQ // QB, QB), F32),
            pltpu.VMEM((8, QB), F32),
            pltpu.SemaphoreType.DMA,
        ],
        compiler_params=params(),
        cost_estimate=cost(4 * SEQ * SEQ * HEAD_DIM, 5_000_000, SEQ * SEQ),
        name="main_attention",
    )(ends, second, hint, notes)


def exchange(block):
    return lax.all_to_all(block, "seq", split_axis=0, concat_axis=0, tiled=True)


def body(
    query,
    key,
    value,
    gain_query,
    gain_key,
    ctrl_query,
    ctrl_key,
    ctrl_value,
    ctrl_gain_query,
    ctrl_gain_key,
    gate_table,
    levels,
    frame_map,
    control_match,
):
    packed = pl.pallas_call(
        pack_ctrl_kernel,
        out_shape=shape(HEADS, ROWS_C, HEAD_DIM),
        in_specs=[whole()] * 7,
        out_specs=whole(),
        compiler_params=params(56),
        cost_estimate=cost(2_000_000, 2_000_000),
        name="pack_ctrl",
    )(
        ctrl_query[0],
        ctrl_key[0],
        ctrl_value[0],
        ctrl_gain_query[None],
        ctrl_gain_key[None],
        frame_map,
        control_match,
    )
    first = exchange(packed)
    packed_main = pl.pallas_call(
        pack_main_kernel,
        out_shape=shape(HEADS, ROWS, HEAD_DIM),
        in_specs=[whole()] * 5,
        out_specs=whole(),
        compiler_params=params(),
        cost_estimate=cost(8_000_000, 6_000_000),
        name="pack_main",
    )(query[0], key[0], value[0], gain_query[None], gain_key[None])
    second = exchange(packed_main)
    places = jnp.concatenate([lax.axis_index("seq")[None].astype(jnp.int32), levels[0]])
    hint, ends, notes = pl.pallas_call(
        ctrl_kernel,
        grid_spec=pltpu.PrefetchScalarGridSpec(
            num_scalar_prefetch=1,
            grid=(1,),
            in_specs=[pl.BlockSpec((LEVELS, HEAD_DIM), lambda i, places: (0, places[0])), whole()],
            out_specs=(whole(), pl.BlockSpec(memory_space=pltpu.SMEM), whole()),
        ),
        out_shape=(
            shape(CTRL, HEAD_DIM),
            shape(FRAMES, dtype=jnp.int32),
            shape(16, 128, dtype=F32),
        ),
        compiler_params=params(),
        cost_estimate=cost(4 * CTRL * CTRL * HEAD_DIM, 1_000_000, CTRL * CTRL),
        name="ctrl_attention",
    )(places, gate_table, first)
    groups = lax.axis_size("grp")
    hint = lax.ppermute(hint, "grp", [((i - 1) % groups, i) for i in range(groups)])
    mixed = run_main(ends, second, hint, notes)
    back = exchange(mixed)
    return pl.pallas_call(
        unpack_kernel,
        out_shape=shape(TOK_DEV, WIDTH),
        in_specs=[whole()],
        out_specs=whole(),
        compiler_params=params(),
        cost_estimate=cost(0, 2_000_000),
        name="unpack",
    )(back)[None]


def solution(mesh):
    return jax.shard_map(
        body,
        mesh=mesh,
        in_specs=(
            P("grp", "seq", None),
            P("grp", "seq", None),
            P("grp", "seq", None),
            P(),
            P(),
            P("grp", "seq", None),
            P("grp", "seq", None),
            P("grp", "seq", None),
            P(),
            P(),
            P(),
            P("grp", None),
            P("grp", "seq"),
            P("grp", "seq"),
        ),
        out_specs=P("grp", "seq", None),
        check_vma=False,
    )
```

```python
import functools
import math

import jax
import jax.numpy as jnp
from jax import lax
from jax.experimental import pallas as pl
from jax.experimental.pallas import tpu as pltpu
from jax.sharding import PartitionSpec as P

HEADS = 32
HEAD_DIM = 128
WIDTH = 4096
TOK_DEV = 128
CTRL_DEV = 32
FRAMES = 8
LEVELS = 16
SEQ = 4096
CTRL = 1024
META = 16
ROW_M = 3 * CTRL_DEV
ROWS_C = ROW_M + META
ROWS = 3 * TOK_DEV
SCALE2 = math.log2(math.e) / math.sqrt(HEAD_DIM)
QB = 512
KB = 1024
PART = 256
WIDE = 8
VR = HEAD_DIM + 16
SAFE = 2.0**100
MIB = 1024 * 1024
F32 = jnp.float32
BF16 = jnp.bfloat16


def params(mib=20):
    return pltpu.CompilerParams(vmem_limit_bytes=mib * MIB)


def whole():
    return pl.BlockSpec(memory_space=pltpu.VMEM)


def rms_round(values, gain):
    wide = values.astype(F32)
    mean_sq = jnp.mean(wide * wide, axis=-1, keepdims=True)
    return (wide * lax.rsqrt(mean_sq + 1e-06) * gain).astype(BF16)


def lay_heads(out_ref, row, values):
    rows = values.shape[0]
    for head in range(HEADS):
        out_ref[head, row : row + rows, :] = values[:, head * HEAD_DIM : (head + 1) * HEAD_DIM]


def pack_ctrl_kernel(cq, ck, cv, gcq, gck, frames, match, out):
    lay_heads(out, 0, rms_round(cq[...], gcq[...]))
    lay_heads(out, CTRL_DEV, rms_round(ck[...], gck[...]))
    lay_heads(out, 2 * CTRL_DEV, cv[...])
    spots = jnp.concatenate([match[...]] * 4, axis=1)
    row = lax.broadcasted_iota(jnp.int32, (META, 128), 0)
    meta = jnp.where(row == 0, frames[...], jnp.where(row == 1, spots // 64, spots % 64))
    meta = jnp.where(row < 3, meta, 0).astype(F32).astype(BF16)
    for head in range(HEADS):
        out[head, ROW_M:, :] = meta


def turned(block):
    return block.astype(F32).T.astype(BF16)


def pack_main_kernel(q, k, v, gq, gk, out, q_norm):
    step = 32
    for at in range(0, TOK_DEV, step):
        q_norm[at : at + step, :] = rms_round(q[at : at + step, :], gq[...])
        lay_heads(out, TOK_DEV + at, rms_round(k[at : at + step, :], gk[...]))
    for head in range(HEADS):
        lanes = slice(head * HEAD_DIM, (head + 1) * HEAD_DIM)
        out[head, :TOK_DEV, :] = turned(q_norm[:, lanes])
        out[head, 2 * TOK_DEV :, :] = turned(v[:, lanes])


def ctrl_kernel(places, table, first, hint, ends, notes):
    meta = first[:, ROW_M:, :].astype(F32)
    frames = meta[:, 0, :]
    for f in range(FRAMES):
        ends[f] = jnp.sum(jnp.where(frames <= f + 0.5, 1.0, 0.0)).astype(jnp.int32)
        notes[8 + f : 9 + f, :] = table[pl.ds(places[1 + f], 1), :]
    spots = (meta[:, 1, :] * 64.0 + meta[:, 2, :]).reshape(8, 4, 128)
    source = lax.broadcasted_iota(jnp.int32, (8, 4, 128), 1)
    lane = lax.broadcasted_iota(jnp.int32, (8, 4, 128), 2)
    notes[:8, :] = jnp.sum(jnp.where(lane // CTRL_DEV == source, spots, 0.0), axis=1)
    keys = first[:, CTRL_DEV : 2 * CTRL_DEV, :].reshape(CTRL, HEAD_DIM)
    values = first[:, 2 * CTRL_DEV : ROW_M, :].reshape(CTRL, HEAD_DIM)
    for part in range(4):
        queries = first[part * 8 : part * 8 + 8, :CTRL_DEV, :].reshape(256, HEAD_DIM)
        scores = lax.dot_general(queries, keys, (((1,), (1,)), ((), ())), preferred_element_type=F32)
        top = jnp.max(scores, axis=1, keepdims=True)
        expo = jnp.exp2((scores - top) * SCALE2)
        total = jnp.sum(expo, axis=1, keepdims=True)
        weights = (expo * (1.0 / total)).astype(BF16)
        rows = jnp.dot(weights, values, preferred_element_type=F32).astype(BF16)
        hint[:, part * 256 : part * 256 + 256] = turned(rows)


def main_kernel(
    ends_ref, second, hint, notes_hbm, out, notes, match, gates, v_t, acc, sums, top_ref, sem
):
    copy = pltpu.make_async_copy(notes_hbm, notes, sem)
    copy.start()
    ends = [ends_ref[f] for f in range(FRAMES)]

    def end_of(token):
        end = jnp.int32(SEQ)
        for f in reversed(range(FRAMES)):
            end = jnp.where(ends[f] > token, ends[f], end)
        return end

    for block in range(HEADS):
        v_t[:HEAD_DIM, block * 128 : block * 128 + 128] = second[block, 2 * TOK_DEV :, :]
    v_t[HEAD_DIM:, :] = jnp.ones((VR - HEAD_DIM, SEQ), BF16)
    copy.wait()
    for g in range(8):
        match[g * 128 : g * 128 + 128, :] = jnp.broadcast_to(notes[g : g + 1, :], (128, 128)).T
        gates[g, :, :] = jnp.broadcast_to(notes[8 + g : 9 + g, :], (128, 128)).T

    def limit_of(base):
        column = lax.broadcasted_iota(jnp.int32, (8, QB), 1) + base
        limit = jnp.full((8, QB), SEQ, jnp.int32)
        for f in reversed(range(FRAMES)):
            limit = jnp.where(ends[f] > column, ends[f], limit)
        return limit[:1, :]

    def queries_of(i):
        per = QB // TOK_DEV
        return jnp.concatenate([second[i * per + n, :TOK_DEV, :] for n in range(per)], axis=1)

    def scores_of(i, j, masked):
        q_t = queries_of(i)
        keys = second[pl.ds(j * (KB // TOK_DEV), KB // TOK_DEV), TOK_DEV : 2 * TOK_DEV, :]
        scores = jnp.dot(keys.reshape(KB, HEAD_DIM), q_t, preferred_element_type=F32)
        return scores

    def visible(limit, j):
        return lax.broadcasted_iota(jnp.int32, (KB, QB), 0) < limit - j * KB

    def values_of(j):
        return v_t[:, pl.ds(pl.multiple_of(j * KB, KB), KB)]

    def finish(i, total):
        base = i * QB
        attn = (total[:HEAD_DIM, :] * (1.0 / total[HEAD_DIM : HEAD_DIM + 1, :])).astype(BF16).astype(F32)
        picks, gate = [], []
        for at in range(0, QB, 128):
            spot = (lax.broadcasted_iota(jnp.int32, (1, 128), 1) + (base + at)).astype(F32)
            picks.append(jnp.where(match[...] == spot, 1.0, 0.0).astype(BF16))
            token = lax.broadcasted_iota(jnp.int32, (HEAD_DIM, 128), 1) + base + at
            level = gates[0]
            for f in range(1, FRAMES):
                level = jnp.where(token >= ends[f - 1], gates[f], level)
            gate.append(level)
        added = jnp.dot(hint[...], jnp.concatenate(picks, axis=1), preferred_element_type=F32)
        mixed = (jnp.concatenate(gate, axis=1) * attn + added).T.astype(BF16)
        rows = QB // TOK_DEV
        out[pl.ds(i * rows, rows), :, :] = mixed.reshape(rows, TOK_DEV, HEAD_DIM)

    def quick_block(i, carry):
        base = i * QB
        limit = limit_of(base)
        q_t = queries_of(i)

        def run(count):
            finish(jnp.maximum(i - 1, 0), acc)
            total = None
            edge = max(0, count - 3 * QB // PART)
            cuts = sorted({0, edge}) + [count]
            for c, d in zip(cuts[:-1], cuts[1:]):
                per = PART // TOK_DEV
                keys = second[c * per : d * per, TOK_DEV : 2 * TOK_DEV, :]
                keys = keys.reshape((d - c) * PART, HEAD_DIM)
                expo = jnp.exp2(jnp.dot(keys, q_t, preferred_element_type=F32) * SCALE2)
                if c >= edge:
                    row = lax.broadcasted_iota(jnp.int32, expo.shape, 0)
                    expo = jnp.where(row < limit - c * PART, expo, 0.0)
                part = jnp.dot(
                    v_t[:, c * PART : d * PART], expo.astype(BF16), preferred_element_type=F32
                )
                total = part if total is None else total + part
            acc[...] = total

        parts = (end_of(base + QB - 1) + PART - 1) // PART
        for count in range(1, SEQ // PART + 1):
            pl.when(parts == count)(functools.partial(run, count))

        sums[pl.ds(i, 1), :] = acc[HEAD_DIM : HEAD_DIM + 1, :]
        return carry

    def full_block(i, carry):
        base = i * QB
        n_all = (end_of(base + QB - 1) + KB - 1) // KB
        limit = limit_of(base)
        acc[...] = jnp.zeros_like(acc)
        top_ref[...] = jnp.full_like(top_ref, -1e30)

        @pl.loop(0, n_all)
        def _(j):
            scores = jnp.where(visible(limit, j), scores_of(i, j, True), -1e30)
            old = top_ref[:1, :]
            new = jnp.maximum(old, jnp.max(scores, axis=0, keepdims=True))
            expo = jnp.exp2((scores - new) * SCALE2).astype(BF16)
            part = jnp.dot(values_of(j), expo, preferred_element_type=F32)
            acc[...] = acc[...] * jnp.exp2((old - new) * SCALE2) + part
            top_ref[...] = jnp.broadcast_to(new, top_ref.shape)

        finish(i, acc)
        return carry

    acc[...] = jnp.ones_like(acc)
    lax.fori_loop(0, SEQ // QB, quick_block, 0)
    finish(SEQ // QB - 1, acc)
    good = (sums[...] > 1.0 / SAFE) & (sums[...] < SAFE)
    count = jnp.sum(jnp.where(good, 1.0, 0.0))

    @pl.when(count < SEQ - 0.5)
    def _():
        lax.fori_loop(0, SEQ // QB, full_block, 0)


def unpack_kernel(rows, out):
    for head in range(HEADS):
        out[:, head * HEAD_DIM : (head + 1) * HEAD_DIM] = rows[head, :, :]


def cost(flops, moved, transcendentals=0):
    return pl.CostEstimate(flops=flops, bytes_accessed=moved, transcendentals=transcendentals)


def shape(*dims, dtype=BF16):
    return jax.ShapeDtypeStruct(dims, dtype)


def run_main(ends, second, hint, notes):
    return pl.pallas_call(
        main_kernel,
        out_shape=shape(HEADS, TOK_DEV, HEAD_DIM),
        in_specs=[pl.BlockSpec(memory_space=pltpu.SMEM)] + [whole()] * 2 + [pl.BlockSpec(memory_space=pltpu.HBM)],
        out_specs=whole(),
        scratch_shapes=[
            pltpu.VMEM((16, 128), F32),
            pltpu.VMEM((CTRL, 128), F32),
            pltpu.VMEM((FRAMES, HEAD_DIM, 128), F32),
            pltpu.VMEM((VR, SEQ), BF16),
            pltpu.VMEM((VR, QB), F32),
            pltpu.VMEM((SEQ // QB, QB), F32),
            pltpu.VMEM((8, QB), F32),
            pltpu.SemaphoreType.DMA,
        ],
        compiler_params=params(),
        cost_estimate=cost(4 * SEQ * SEQ * HEAD_DIM, 5_000_000, SEQ * SEQ),
        name="main_attention",
    )(ends, second, hint, notes)


def exchange(block):
    return lax.all_to_all(block, "seq", split_axis=0, concat_axis=0, tiled=True)


def body(
    query,
    key,
    value,
    gain_query,
    gain_key,
    ctrl_query,
    ctrl_key,
    ctrl_value,
    ctrl_gain_query,
    ctrl_gain_key,
    gate_table,
    levels,
    frame_map,
    control_match,
):
    packed = pl.pallas_call(
        pack_ctrl_kernel,
        out_shape=shape(HEADS, ROWS_C, HEAD_DIM),
        in_specs=[whole()] * 7,
        out_specs=whole(),
        compiler_params=params(56),
        cost_estimate=cost(2_000_000, 2_000_000),
        name="pack_ctrl",
    )(
        ctrl_query[0],
        ctrl_key[0],
        ctrl_value[0],
        ctrl_gain_query[None],
        ctrl_gain_key[None],
        frame_map,
        control_match,
    )
    first = exchange(packed)
    packed_main = pl.pallas_call(
        pack_main_kernel,
        out_shape=shape(HEADS, ROWS, HEAD_DIM),
        in_specs=[whole()] * 5,
        out_specs=whole(),
        scratch_shapes=[pltpu.VMEM((TOK_DEV, WIDTH), BF16)],
        compiler_params=params(),
        cost_estimate=cost(8_000_000, 6_000_000),
        name="pack_main",
    )(query[0], key[0], value[0], gain_query[None], gain_key[None])
    second = exchange(packed_main)
    places = jnp.concatenate([lax.axis_index("seq")[None].astype(jnp.int32), levels[0]])
    hint, ends, notes = pl.pallas_call(
        ctrl_kernel,
        grid_spec=pltpu.PrefetchScalarGridSpec(
            num_scalar_prefetch=1,
            grid=(1,),
            in_specs=[pl.BlockSpec((LEVELS, HEAD_DIM), lambda i, places: (0, places[0])), whole()],
            out_specs=(whole(), pl.BlockSpec(memory_space=pltpu.SMEM), whole()),
        ),
        out_shape=(
            shape(HEAD_DIM, CTRL),
            shape(FRAMES, dtype=jnp.int32),
            shape(16, 128, dtype=F32),
        ),
        compiler_params=params(),
        cost_estimate=cost(4 * CTRL * CTRL * HEAD_DIM, 1_000_000, CTRL * CTRL),
        name="ctrl_attention",
    )(places, gate_table, first)
    groups = lax.axis_size("grp")
    hint = lax.ppermute(hint, "grp", [((i - 1) % groups, i) for i in range(groups)])
    mixed = run_main(ends, second, hint, notes)
    back = exchange(mixed)
    return pl.pallas_call(
        unpack_kernel,
        out_shape=shape(TOK_DEV, WIDTH),
        in_specs=[whole()],
        out_specs=whole(),
        compiler_params=params(),
        cost_estimate=cost(0, 2_000_000),
        name="unpack",
    )(back)[None]


def solution(mesh):
    return jax.shard_map(
        body,
        mesh=mesh,
        in_specs=(
            P("grp", "seq", None),
            P("grp", "seq", None),
            P("grp", "seq", None),
            P(),
            P(),
            P("grp", "seq", None),
            P("grp", "seq", None),
            P("grp", "seq", None),
            P(),
            P(),
            P(),
            P("grp", None),
            P("grp", "seq"),
            P("grp", "seq"),
        ),
        out_specs=P("grp", "seq", None),
        check_vma=False,
    )
```

```python
import functools
import math

import jax
import jax.numpy as jnp
from jax import lax
from jax.experimental import pallas as pl
from jax.experimental.pallas import tpu as pltpu
from jax.sharding import PartitionSpec as P

HEADS = 32
HEAD_DIM = 128
WIDTH = 4096
TOK_DEV = 128
CTRL_DEV = 32
FRAMES = 8
LEVELS = 16
SEQ = 4096
CTRL = 1024
META = 16
ROW_M = 3 * CTRL_DEV
ROWS_C = ROW_M + META
ROWS = 3 * TOK_DEV
SCALE2 = math.log2(math.e) / math.sqrt(HEAD_DIM)
QB = 512
KB = 1024
PART = 256
VR = HEAD_DIM + 16
SAFE = 2.0**100
MIB = 1024 * 1024
F32 = jnp.float32
BF16 = jnp.bfloat16


def params(mib=20):
    return pltpu.CompilerParams(vmem_limit_bytes=mib * MIB)


def whole():
    return pl.BlockSpec(memory_space=pltpu.VMEM)


def rms_round(values, gain):
    wide = values.astype(F32)
    mean_sq = jnp.mean(wide * wide, axis=-1, keepdims=True)
    return (wide * lax.rsqrt(mean_sq + 1e-06) * gain).astype(BF16)


def lay_heads(out_ref, row, values):
    rows = values.shape[0]
    for head in range(HEADS):
        out_ref[head, row : row + rows, :] = values[:, head * HEAD_DIM : (head + 1) * HEAD_DIM]


def pack_ctrl_kernel(cq, ck, cv, gcq, gck, frames, match, out):
    lay_heads(out, 0, rms_round(cq[...], gcq[...]))
    lay_heads(out, CTRL_DEV, rms_round(ck[...], gck[...]))
    lay_heads(out, 2 * CTRL_DEV, cv[...])
    spots = jnp.concatenate([match[...]] * 4, axis=1)
    row = lax.broadcasted_iota(jnp.int32, (META, 128), 0)
    meta = jnp.where(row == 0, frames[...], jnp.where(row == 1, spots // 64, spots % 64))
    meta = jnp.where(row < 3, meta, 0).astype(F32).astype(BF16)
    for head in range(HEADS):
        out[head, ROW_M:, :] = meta


def turned(block):
    return block.astype(F32).T.astype(BF16)


def pack_main_kernel(q, k, v, gq, gk, out, q_norm):
    step = 32
    for at in range(0, TOK_DEV, step):
        q_norm[at : at + step, :] = rms_round(q[at : at + step, :], gq[...])
        lay_heads(out, TOK_DEV + at, rms_round(k[at : at + step, :], gk[...]))
    for head in range(HEADS):
        lanes = slice(head * HEAD_DIM, (head + 1) * HEAD_DIM)
        out[head, :TOK_DEV, :] = turned(q_norm[:, lanes])
        out[head, 2 * TOK_DEV :, :] = turned(v[:, lanes])


def ctrl_kernel(places, table, first, hint, ends, notes):
    meta = first[:, ROW_M:, :].astype(F32)
    frames = meta[:, 0, :]
    for f in range(FRAMES):
        ends[f] = jnp.sum(jnp.where(frames <= f + 0.5, 1.0, 0.0)).astype(jnp.int32)
        notes[8 + f : 9 + f, :] = table[pl.ds(places[1 + f], 1), :]
    spots = (meta[:, 1, :] * 64.0 + meta[:, 2, :]).reshape(8, 4, 128)
    source = lax.broadcasted_iota(jnp.int32, (8, 4, 128), 1)
    lane = lax.broadcasted_iota(jnp.int32, (8, 4, 128), 2)
    notes[:8, :] = jnp.sum(jnp.where(lane // CTRL_DEV == source, spots, 0.0), axis=1)
    keys = first[:, CTRL_DEV : 2 * CTRL_DEV, :].reshape(CTRL, HEAD_DIM)
    values = first[:, 2 * CTRL_DEV : ROW_M, :].reshape(CTRL, HEAD_DIM)
    for part in range(4):
        queries = first[part * 8 : part * 8 + 8, :CTRL_DEV, :].reshape(256, HEAD_DIM)
        scores = lax.dot_general(queries, keys, (((1,), (1,)), ((), ())), preferred_element_type=F32)
        top = jnp.max(scores, axis=1, keepdims=True)
        expo = jnp.exp2((scores - top) * SCALE2)
        total = jnp.sum(expo, axis=1, keepdims=True)
        weights = (expo * (1.0 / total)).astype(BF16)
        rows = jnp.dot(weights, values, preferred_element_type=F32).astype(BF16)
        hint[:, part * 256 : part * 256 + 256] = turned(rows)


def main_kernel(
    ends_ref, second, hint, notes_hbm, out, notes, match, gates, v_t, k_mark, acc, sums, top_ref, sem
):
    copy = pltpu.make_async_copy(notes_hbm, notes, sem)
    copy.start()
    ends = [ends_ref[f] for f in range(FRAMES)]

    def end_of(token):
        end = jnp.int32(SEQ)
        for f in reversed(range(FRAMES)):
            end = jnp.where(ends[f] > token, ends[f], end)
        return end

    for block in range(HEADS):
        v_t[:HEAD_DIM, block * 128 : block * 128 + 128] = second[block, 2 * TOK_DEV :, :]
    lane = lax.broadcasted_iota(jnp.int32, (1, 128), 1)
    marks = jnp.full((1, 128), SEQ, jnp.int32)
    for f in range(FRAMES):
        marks = jnp.where(lane == f, ends[f], marks)
    for block in range(HEADS):
        rows = slice(block * TOK_DEV, (block + 1) * TOK_DEV)
        k_mark[rows, :HEAD_DIM] = second[block, TOK_DEV : 2 * TOK_DEV, :]
        token = lax.broadcasted_iota(jnp.int32, (TOK_DEV, 128), 0) + block * TOK_DEV
        k_mark[rows, HEAD_DIM:] = jnp.where(token >= marks, 1.0, 0.0).astype(BF16)
    v_t[HEAD_DIM:, :] = jnp.ones((VR - HEAD_DIM, SEQ), BF16)
    copy.wait()
    for g in range(8):
        match[g * 128 : g * 128 + 128, :] = jnp.broadcast_to(notes[g : g + 1, :], (128, 128)).T
        gates[g, :, :] = jnp.broadcast_to(notes[8 + g : 9 + g, :], (128, 128)).T

    def limit_of(base):
        column = lax.broadcasted_iota(jnp.int32, (8, QB), 1) + base
        limit = jnp.full((8, QB), SEQ, jnp.int32)
        for f in reversed(range(FRAMES)):
            limit = jnp.where(ends[f] > column, ends[f], limit)
        return limit[:1, :]

    def queries_of(i):
        per = QB // TOK_DEV
        return jnp.concatenate([second[i * per + n, :TOK_DEV, :] for n in range(per)], axis=1)

    def scores_of(i, j, masked):
        q_t = queries_of(i)
        keys = second[pl.ds(j * (KB // TOK_DEV), KB // TOK_DEV), TOK_DEV : 2 * TOK_DEV, :]
        scores = jnp.dot(keys.reshape(KB, HEAD_DIM), q_t, preferred_element_type=F32)
        return scores

    def visible(limit, j):
        return lax.broadcasted_iota(jnp.int32, (KB, QB), 0) < limit - j * KB

    def values_of(j):
        return v_t[:, pl.ds(pl.multiple_of(j * KB, KB), KB)]

    def finish(i, total):
        base = i * QB
        attn = (total[:HEAD_DIM, :] * (1.0 / total[HEAD_DIM : HEAD_DIM + 1, :])).astype(BF16).astype(F32)
        picks, gate = [], []
        for at in range(0, QB, 128):
            spot = (lax.broadcasted_iota(jnp.int32, (1, 128), 1) + (base + at)).astype(F32)
            picks.append(jnp.where(match[...] == spot, 1.0, 0.0).astype(BF16))
            token = lax.broadcasted_iota(jnp.int32, (HEAD_DIM, 128), 1) + base + at
            level = gates[0]
            for f in range(1, FRAMES):
                level = jnp.where(token >= ends[f - 1], gates[f], level)
            gate.append(level)
        added = jnp.dot(hint[...], jnp.concatenate(picks, axis=1), preferred_element_type=F32)
        mixed = (jnp.concatenate(gate, axis=1) * attn + added).T.astype(BF16)
        rows = QB // TOK_DEV
        out[pl.ds(i * rows, rows), :, :] = mixed.reshape(rows, TOK_DEV, HEAD_DIM)

    def quick_block(i, carry):
        base = i * QB
        q_t = queries_of(i)
        column = lax.broadcasted_iota(jnp.int32, (16, QB), 1) + base
        frame = jnp.zeros((16, QB), jnp.int32)
        for f in range(FRAMES - 1):
            frame = jnp.where(column >= ends[f], f + 1, frame)
        hide = jnp.where(lax.broadcasted_iota(jnp.int32, (16, QB), 0) == frame, -1e30, 0.0)
        q_mark = jnp.concatenate(
            [q_t, hide.astype(BF16), jnp.zeros((HEAD_DIM - 16, QB), BF16)], axis=0
        )

        def run(count):
            finish(jnp.maximum(i - 1, 0), acc)
            keys = k_mark[: count * PART, :]
            expo = jnp.exp2(jnp.dot(keys, q_mark, preferred_element_type=F32) * SCALE2)
            acc[...] = jnp.dot(
                v_t[:, : count * PART], expo.astype(BF16), preferred_element_type=F32
            )

        parts = (end_of(base + QB - 1) + PART - 1) // PART
        for count in range(1, SEQ // PART + 1):
            pl.when(parts == count)(functools.partial(run, count))

        sums[pl.ds(i, 1), :] = acc[HEAD_DIM : HEAD_DIM + 1, :]
        return carry

    def full_block(i, carry):
        base = i * QB
        n_all = (end_of(base + QB - 1) + KB - 1) // KB
        limit = limit_of(base)
        acc[...] = jnp.zeros_like(acc)
        top_ref[...] = jnp.full_like(top_ref, -1e30)

        @pl.loop(0, n_all)
        def _(j):
            scores = jnp.where(visible(limit, j), scores_of(i, j, True), -1e30)
            old = top_ref[:1, :]
            new = jnp.maximum(old, jnp.max(scores, axis=0, keepdims=True))
            expo = jnp.exp2((scores - new) * SCALE2).astype(BF16)
            part = jnp.dot(values_of(j), expo, preferred_element_type=F32)
            acc[...] = acc[...] * jnp.exp2((old - new) * SCALE2) + part
            top_ref[...] = jnp.broadcast_to(new, top_ref.shape)

        finish(i, acc)
        return carry

    acc[...] = jnp.ones_like(acc)
    lax.fori_loop(0, SEQ // QB, quick_block, 0)
    finish(SEQ // QB - 1, acc)
    good = (sums[...] > 1.0 / SAFE) & (sums[...] < SAFE)
    count = jnp.sum(jnp.where(good, 1.0, 0.0))

    @pl.when(count < SEQ - 0.5)
    def _():
        lax.fori_loop(0, SEQ // QB, full_block, 0)


def unpack_kernel(rows, out):
    for head in range(HEADS):
        out[:, head * HEAD_DIM : (head + 1) * HEAD_DIM] = rows[head, :, :]


def cost(flops, moved, transcendentals=0):
    return pl.CostEstimate(flops=flops, bytes_accessed=moved, transcendentals=transcendentals)


def shape(*dims, dtype=BF16):
    return jax.ShapeDtypeStruct(dims, dtype)


def run_main(ends, second, hint, notes):
    return pl.pallas_call(
        main_kernel,
        out_shape=shape(HEADS, TOK_DEV, HEAD_DIM),
        in_specs=[pl.BlockSpec(memory_space=pltpu.SMEM)] + [whole()] * 2 + [pl.BlockSpec(memory_space=pltpu.HBM)],
        out_specs=whole(),
        scratch_shapes=[
            pltpu.VMEM((16, 128), F32),
            pltpu.VMEM((CTRL, 128), F32),
            pltpu.VMEM((FRAMES, HEAD_DIM, 128), F32),
            pltpu.VMEM((VR, SEQ), BF16),
            pltpu.VMEM((SEQ, 2 * HEAD_DIM), BF16),
            pltpu.VMEM((VR, QB), F32),
            pltpu.VMEM((SEQ // QB, QB), F32),
            pltpu.VMEM((8, QB), F32),
            pltpu.SemaphoreType.DMA,
        ],
        compiler_params=params(),
        cost_estimate=cost(4 * SEQ * SEQ * HEAD_DIM, 5_000_000, SEQ * SEQ),
        name="main_attention",
    )(ends, second, hint, notes)


def exchange(block):
    return lax.all_to_all(block, "seq", split_axis=0, concat_axis=0, tiled=True)


def body(
    query,
    key,
    value,
    gain_query,
    gain_key,
    ctrl_query,
    ctrl_key,
    ctrl_value,
    ctrl_gain_query,
    ctrl_gain_key,
    gate_table,
    levels,
    frame_map,
    control_match,
):
    packed = pl.pallas_call(
        pack_ctrl_kernel,
        out_shape=shape(HEADS, ROWS_C, HEAD_DIM),
        in_specs=[whole()] * 7,
        out_specs=whole(),
        compiler_params=params(56),
        cost_estimate=cost(2_000_000, 2_000_000),
        name="pack_ctrl",
    )(
        ctrl_query[0],
        ctrl_key[0],
        ctrl_value[0],
        ctrl_gain_query[None],
        ctrl_gain_key[None],
        frame_map,
        control_match,
    )
    first = exchange(packed)
    packed_main = pl.pallas_call(
        pack_main_kernel,
        out_shape=shape(HEADS, ROWS, HEAD_DIM),
        in_specs=[whole()] * 5,
        out_specs=whole(),
        scratch_shapes=[pltpu.VMEM((TOK_DEV, WIDTH), BF16)],
        compiler_params=params(),
        cost_estimate=cost(8_000_000, 6_000_000),
        name="pack_main",
    )(query[0], key[0], value[0], gain_query[None], gain_key[None])
    second = exchange(packed_main)
    places = jnp.concatenate([lax.axis_index("seq")[None].astype(jnp.int32), levels[0]])
    hint, ends, notes = pl.pallas_call(
        ctrl_kernel,
        grid_spec=pltpu.PrefetchScalarGridSpec(
            num_scalar_prefetch=1,
            grid=(1,),
            in_specs=[pl.BlockSpec((LEVELS, HEAD_DIM), lambda i, places: (0, places[0])), whole()],
            out_specs=(whole(), pl.BlockSpec(memory_space=pltpu.SMEM), whole()),
        ),
        out_shape=(
            shape(HEAD_DIM, CTRL),
            shape(FRAMES, dtype=jnp.int32),
            shape(16, 128, dtype=F32),
        ),
        compiler_params=params(),
        cost_estimate=cost(4 * CTRL * CTRL * HEAD_DIM, 1_000_000, CTRL * CTRL),
        name="ctrl_attention",
    )(places, gate_table, first)
    groups = lax.axis_size("grp")
    hint = lax.ppermute(hint, "grp", [((i - 1) % groups, i) for i in range(groups)])
    mixed = run_main(ends, second, hint, notes)
    back = exchange(mixed)
    return pl.pallas_call(
        unpack_kernel,
        out_shape=shape(TOK_DEV, WIDTH),
        in_specs=[whole()],
        out_specs=whole(),
        compiler_params=params(),
        cost_estimate=cost(0, 2_000_000),
        name="unpack",
    )(back)[None]


def solution(mesh):
    return jax.shard_map(
        body,
        mesh=mesh,
        in_specs=(
            P("grp", "seq", None),
            P("grp", "seq", None),
            P("grp", "seq", None),
            P(),
            P(),
            P("grp", "seq", None),
            P("grp", "seq", None),
            P("grp", "seq", None),
            P(),
            P(),
            P(),
            P("grp", None),
            P("grp", "seq"),
            P("grp", "seq"),
        ),
        out_specs=P("grp", "seq", None),
        check_vma=False,
    )
```

```python
import math

import jax
import jax.numpy as jnp
from jax import lax
from jax.experimental import pallas as pl
from jax.experimental.pallas import tpu as pltpu
from jax.sharding import PartitionSpec as P

HEADS = 32
HEAD_DIM = 128
WIDTH = 4096
TOK_DEV = 128
CTRL_DEV = 32
FRAMES = 8
LEVELS = 16
SEQ = 4096
CTRL = 1024
META = 16
ROW_M = 3 * CTRL_DEV
ROWS_C = ROW_M + META
ROWS = 3 * TOK_DEV
SCALE2 = math.log2(math.e) / math.sqrt(HEAD_DIM)
QB = 512
KB = 1024
PART = 256
VR = HEAD_DIM + 16
SAFE = 2.0**100
MIB = 1024 * 1024
F32 = jnp.float32
BF16 = jnp.bfloat16


def params(mib=20):
    return pltpu.CompilerParams(vmem_limit_bytes=mib * MIB)


def whole():
    return pl.BlockSpec(memory_space=pltpu.VMEM)


def rms_round(values, gain):
    wide = values.astype(F32)
    mean_sq = jnp.mean(wide * wide, axis=-1, keepdims=True)
    return (wide * lax.rsqrt(mean_sq + 1e-06) * gain).astype(BF16)


def lay_heads(out_ref, row, values):
    rows = values.shape[0]
    for head in range(HEADS):
        out_ref[head, row : row + rows, :] = values[:, head * HEAD_DIM : (head + 1) * HEAD_DIM]


def pack_ctrl_kernel(cq, ck, cv, gcq, gck, frames, match, out):
    lay_heads(out, 0, rms_round(cq[...], gcq[...]))
    lay_heads(out, CTRL_DEV, rms_round(ck[...], gck[...]))
    lay_heads(out, 2 * CTRL_DEV, cv[...])
    spots = jnp.concatenate([match[...]] * 4, axis=1)
    row = lax.broadcasted_iota(jnp.int32, (META, 128), 0)
    meta = jnp.where(row == 0, frames[...], jnp.where(row == 1, spots // 64, spots % 64))
    meta = jnp.where(row < 3, meta, 0).astype(F32).astype(BF16)
    for head in range(HEADS):
        out[head, ROW_M:, :] = meta


def turned(block):
    return block.astype(F32).T.astype(BF16)


def pack_main_kernel(q, k, v, gq, gk, out, q_norm):
    step = 32
    for at in range(0, TOK_DEV, step):
        q_norm[at : at + step, :] = rms_round(q[at : at + step, :], gq[...])
        lay_heads(out, TOK_DEV + at, rms_round(k[at : at + step, :], gk[...]))
    for head in range(HEADS):
        lanes = slice(head * HEAD_DIM, (head + 1) * HEAD_DIM)
        out[head, :TOK_DEV, :] = turned(q_norm[:, lanes])
        out[head, 2 * TOK_DEV :, :] = turned(v[:, lanes])


def ctrl_kernel(places, table, first, hint, ends, notes):
    meta = first[:, ROW_M:, :].astype(F32)
    frames = meta[:, 0, :]
    for f in range(FRAMES):
        ends[f] = jnp.sum(jnp.where(frames <= f + 0.5, 1.0, 0.0)).astype(jnp.int32)
        notes[8 + f : 9 + f, :] = table[pl.ds(places[1 + f], 1), :]
    spots = (meta[:, 1, :] * 64.0 + meta[:, 2, :]).reshape(8, 4, 128)
    source = lax.broadcasted_iota(jnp.int32, (8, 4, 128), 1)
    lane = lax.broadcasted_iota(jnp.int32, (8, 4, 128), 2)
    notes[:8, :] = jnp.sum(jnp.where(lane // CTRL_DEV == source, spots, 0.0), axis=1)
    keys = first[:, CTRL_DEV : 2 * CTRL_DEV, :].reshape(CTRL, HEAD_DIM)
    values = first[:, 2 * CTRL_DEV : ROW_M, :].reshape(CTRL, HEAD_DIM)
    for part in range(4):
        queries = first[part * 8 : part * 8 + 8, :CTRL_DEV, :].reshape(256, HEAD_DIM)
        scores = lax.dot_general(queries, keys, (((1,), (1,)), ((), ())), preferred_element_type=F32)
        top = jnp.max(scores, axis=1, keepdims=True)
        expo = jnp.exp2((scores - top) * SCALE2)
        total = jnp.sum(expo, axis=1, keepdims=True)
        weights = (expo * (1.0 / total)).astype(BF16)
        rows = jnp.dot(weights, values, preferred_element_type=F32).astype(BF16)
        hint[:, part * 256 : part * 256 + 256] = turned(rows)


def main_kernel(
    ends_ref, second, hint, notes_hbm, out, notes, match, gates, v_t, k_mark, acc, sums, top_ref, sem
):
    copy = pltpu.make_async_copy(notes_hbm, notes, sem)
    copy.start()
    ends = [ends_ref[f] for f in range(FRAMES)]

    def end_of(token):
        end = jnp.int32(SEQ)
        for f in reversed(range(FRAMES)):
            end = jnp.where(ends[f] > token, ends[f], end)
        return end

    for block in range(HEADS):
        v_t[:HEAD_DIM, block * 128 : block * 128 + 128] = second[block, 2 * TOK_DEV :, :]
    lane = lax.broadcasted_iota(jnp.int32, (1, 128), 1)
    marks = jnp.full((1, 128), SEQ, jnp.int32)
    for f in range(FRAMES):
        marks = jnp.where(lane == f, ends[f], marks)
    for block in range(HEADS):
        rows = slice(block * TOK_DEV, (block + 1) * TOK_DEV)
        k_mark[rows, :HEAD_DIM] = second[block, TOK_DEV : 2 * TOK_DEV, :]
        token = lax.broadcasted_iota(jnp.int32, (TOK_DEV, 128), 0) + block * TOK_DEV
        k_mark[rows, HEAD_DIM:] = jnp.where(token >= marks, 1.0, 0.0).astype(BF16)
    v_t[HEAD_DIM:, :] = jnp.ones((VR - HEAD_DIM, SEQ), BF16)
    copy.wait()
    for g in range(8):
        match[g * 128 : g * 128 + 128, :] = jnp.broadcast_to(notes[g : g + 1, :], (128, 128)).T
        gates[g, :, :] = jnp.broadcast_to(notes[8 + g : 9 + g, :], (128, 128)).T

    def limit_of(base):
        column = lax.broadcasted_iota(jnp.int32, (8, QB), 1) + base
        limit = jnp.full((8, QB), SEQ, jnp.int32)
        for f in reversed(range(FRAMES)):
            limit = jnp.where(ends[f] > column, ends[f], limit)
        return limit[:1, :]

    def queries_of(i):
        per = QB // TOK_DEV
        return jnp.concatenate([second[i * per + n, :TOK_DEV, :] for n in range(per)], axis=1)

    def scores_of(i, j, masked):
        q_t = queries_of(i)
        keys = second[pl.ds(j * (KB // TOK_DEV), KB // TOK_DEV), TOK_DEV : 2 * TOK_DEV, :]
        scores = jnp.dot(keys.reshape(KB, HEAD_DIM), q_t, preferred_element_type=F32)
        return scores

    def visible(limit, j):
        return lax.broadcasted_iota(jnp.int32, (KB, QB), 0) < limit - j * KB

    def values_of(j):
        return v_t[:, pl.ds(pl.multiple_of(j * KB, KB), KB)]

    def finish(i, total):
        base = i * QB
        attn = (total[:HEAD_DIM, :] * (1.0 / total[HEAD_DIM : HEAD_DIM + 1, :])).astype(BF16).astype(F32)
        picks, gate = [], []
        for at in range(0, QB, 128):
            spot = (lax.broadcasted_iota(jnp.int32, (1, 128), 1) + (base + at)).astype(F32)
            picks.append(jnp.where(match[...] == spot, 1.0, 0.0).astype(BF16))
            token = lax.broadcasted_iota(jnp.int32, (HEAD_DIM, 128), 1) + base + at
            level = gates[0]
            for f in range(1, FRAMES):
                level = jnp.where(token >= ends[f - 1], gates[f], level)
            gate.append(level)
        added = jnp.dot(hint[...], jnp.concatenate(picks, axis=1), preferred_element_type=F32)
        mixed = (jnp.concatenate(gate, axis=1) * attn + added).T.astype(BF16)
        rows = QB // TOK_DEV
        out[pl.ds(i * rows, rows), :, :] = mixed.reshape(rows, TOK_DEV, HEAD_DIM)

    def quick_block(i, carry):
        base = i * QB
        q_t = queries_of(i)
        column = lax.broadcasted_iota(jnp.int32, (16, QB), 1) + base
        frame = jnp.zeros((16, QB), jnp.int32)
        for f in range(FRAMES - 1):
            frame = jnp.where(column >= ends[f], f + 1, frame)
        hide = jnp.where(lax.broadcasted_iota(jnp.int32, (16, QB), 0) == frame, -1e30, 0.0)
        q_mark = jnp.concatenate(
            [q_t, hide.astype(BF16), jnp.zeros((HEAD_DIM - 16, QB), BF16)], axis=0
        )

        def run(count):
            finish(jnp.maximum(i - 1, 0), acc)
            keys = k_mark[: count * PART, :]
            expo = jnp.exp2(jnp.dot(keys, q_mark, preferred_element_type=F32) * SCALE2)
            acc[...] = jnp.dot(
                v_t[:, : count * PART], expo.astype(BF16), preferred_element_type=F32
            )

        parts = (end_of(base + QB - 1) + PART - 1) // PART
        def choose(low, high):
            if low == high:
                run(low)
                return
            middle = (low + high) // 2
            lax.cond(
                parts <= middle, lambda: choose(low, middle), lambda: choose(middle + 1, high)
            )

        choose(1, SEQ // PART)

        sums[pl.ds(i, 1), :] = acc[HEAD_DIM : HEAD_DIM + 1, :]
        return carry

    def full_block(i, carry):
        base = i * QB
        n_all = (end_of(base + QB - 1) + KB - 1) // KB
        limit = limit_of(base)
        acc[...] = jnp.zeros_like(acc)
        top_ref[...] = jnp.full_like(top_ref, -1e30)

        @pl.loop(0, n_all)
        def _(j):
            scores = jnp.where(visible(limit, j), scores_of(i, j, True), -1e30)
            old = top_ref[:1, :]
            new = jnp.maximum(old, jnp.max(scores, axis=0, keepdims=True))
            expo = jnp.exp2((scores - new) * SCALE2).astype(BF16)
            part = jnp.dot(values_of(j), expo, preferred_element_type=F32)
            acc[...] = acc[...] * jnp.exp2((old - new) * SCALE2) + part
            top_ref[...] = jnp.broadcast_to(new, top_ref.shape)

        finish(i, acc)
        return carry

    acc[...] = jnp.ones_like(acc)
    lax.fori_loop(0, SEQ // QB, quick_block, 0)
    finish(SEQ // QB - 1, acc)
    good = (sums[...] > 1.0 / SAFE) & (sums[...] < SAFE)
    count = jnp.sum(jnp.where(good, 1.0, 0.0))

    @pl.when(count < SEQ - 0.5)
    def _():
        lax.fori_loop(0, SEQ // QB, full_block, 0)


def unpack_kernel(rows, out):
    for head in range(HEADS):
        out[:, head * HEAD_DIM : (head + 1) * HEAD_DIM] = rows[head, :, :]


def cost(flops, moved, transcendentals=0):
    return pl.CostEstimate(flops=flops, bytes_accessed=moved, transcendentals=transcendentals)


def shape(*dims, dtype=BF16):
    return jax.ShapeDtypeStruct(dims, dtype)


def run_main(ends, second, hint, notes):
    return pl.pallas_call(
        main_kernel,
        out_shape=shape(HEADS, TOK_DEV, HEAD_DIM),
        in_specs=[pl.BlockSpec(memory_space=pltpu.SMEM)] + [whole()] * 2 + [pl.BlockSpec(memory_space=pltpu.HBM)],
        out_specs=whole(),
        scratch_shapes=[
            pltpu.VMEM((16, 128), F32),
            pltpu.VMEM((CTRL, 128), F32),
            pltpu.VMEM((FRAMES, HEAD_DIM, 128), F32),
            pltpu.VMEM((VR, SEQ), BF16),
            pltpu.VMEM((SEQ, 2 * HEAD_DIM), BF16),
            pltpu.VMEM((VR, QB), F32),
            pltpu.VMEM((SEQ // QB, QB), F32),
            pltpu.VMEM((8, QB), F32),
            pltpu.SemaphoreType.DMA,
        ],
        compiler_params=params(),
        cost_estimate=cost(4 * SEQ * SEQ * HEAD_DIM, 5_000_000, SEQ * SEQ),
        name="main_attention",
    )(ends, second, hint, notes)


def exchange(block):
    return lax.all_to_all(block, "seq", split_axis=0, concat_axis=0, tiled=True)


def body(
    query,
    key,
    value,
    gain_query,
    gain_key,
    ctrl_query,
    ctrl_key,
    ctrl_value,
    ctrl_gain_query,
    ctrl_gain_key,
    gate_table,
    levels,
    frame_map,
    control_match,
):
    packed = pl.pallas_call(
        pack_ctrl_kernel,
        out_shape=shape(HEADS, ROWS_C, HEAD_DIM),
        in_specs=[whole()] * 7,
        out_specs=whole(),
        compiler_params=params(56),
        cost_estimate=cost(2_000_000, 2_000_000),
        name="pack_ctrl",
    )(
        ctrl_query[0],
        ctrl_key[0],
        ctrl_value[0],
        ctrl_gain_query[None],
        ctrl_gain_key[None],
        frame_map,
        control_match,
    )
    first = exchange(packed)
    packed_main = pl.pallas_call(
        pack_main_kernel,
        out_shape=shape(HEADS, ROWS, HEAD_DIM),
        in_specs=[whole()] * 5,
        out_specs=whole(),
        scratch_shapes=[pltpu.VMEM((TOK_DEV, WIDTH), BF16)],
        compiler_params=params(),
        cost_estimate=cost(8_000_000, 6_000_000),
        name="pack_main",
    )(query[0], key[0], value[0], gain_query[None], gain_key[None])
    second = exchange(packed_main)
    places = jnp.concatenate([lax.axis_index("seq")[None].astype(jnp.int32), levels[0]])
    hint, ends, notes = pl.pallas_call(
        ctrl_kernel,
        grid_spec=pltpu.PrefetchScalarGridSpec(
            num_scalar_prefetch=1,
            grid=(1,),
            in_specs=[pl.BlockSpec((LEVELS, HEAD_DIM), lambda i, places: (0, places[0])), whole()],
            out_specs=(whole(), pl.BlockSpec(memory_space=pltpu.SMEM), whole()),
        ),
        out_shape=(
            shape(HEAD_DIM, CTRL),
            shape(FRAMES, dtype=jnp.int32),
            shape(16, 128, dtype=F32),
        ),
        compiler_params=params(),
        cost_estimate=cost(4 * CTRL * CTRL * HEAD_DIM, 1_000_000, CTRL * CTRL),
        name="ctrl_attention",
    )(places, gate_table, first)
    groups = lax.axis_size("grp")
    hint = lax.ppermute(hint, "grp", [((i - 1) % groups, i) for i in range(groups)])
    mixed = run_main(ends, second, hint, notes)
    back = exchange(mixed)
    return pl.pallas_call(
        unpack_kernel,
        out_shape=shape(TOK_DEV, WIDTH),
        in_specs=[whole()],
        out_specs=whole(),
        compiler_params=params(),
        cost_estimate=cost(0, 2_000_000),
        name="unpack",
    )(back)[None]


def solution(mesh):
    return jax.shard_map(
        body,
        mesh=mesh,
        in_specs=(
            P("grp", "seq", None),
            P("grp", "seq", None),
            P("grp", "seq", None),
            P(),
            P(),
            P("grp", "seq", None),
            P("grp", "seq", None),
            P("grp", "seq", None),
            P(),
            P(),
            P(),
            P("grp", None),
            P("grp", "seq"),
            P("grp", "seq"),
        ),
        out_specs=P("grp", "seq", None),
        check_vma=False,
    )
```

```python
import math

import jax
import jax.numpy as jnp
from jax import lax
from jax.experimental import pallas as pl
from jax.experimental.pallas import tpu as pltpu
from jax.sharding import PartitionSpec as P

HEADS = 32
HEAD_DIM = 128
WIDTH = 4096
TOK_DEV = 128
CTRL_DEV = 32
FRAMES = 8
LEVELS = 16
SEQ = 4096
CTRL = 1024
META = 16
ROW_M = 3 * CTRL_DEV
ROWS_C = ROW_M + META
ROWS = 3 * TOK_DEV
SCALE2 = math.log2(math.e) / math.sqrt(HEAD_DIM)
QB = 512
KB = 1024
PART = 256
VR = HEAD_DIM + 16
SAFE = 2.0**100
MIB = 1024 * 1024
F32 = jnp.float32
BF16 = jnp.bfloat16


def params(mib=20):
    return pltpu.CompilerParams(vmem_limit_bytes=mib * MIB)


def whole():
    return pl.BlockSpec(memory_space=pltpu.VMEM)


def rms_round(values, gain):
    wide = values.astype(F32)
    mean_sq = jnp.mean(wide * wide, axis=-1, keepdims=True)
    return (wide * lax.rsqrt(mean_sq + 1e-06) * gain).astype(BF16)


def lay_heads(out_ref, row, values):
    rows = values.shape[0]
    for head in range(HEADS):
        out_ref[head, row : row + rows, :] = values[:, head * HEAD_DIM : (head + 1) * HEAD_DIM]


def pack_ctrl_kernel(cq, ck, cv, gcq, gck, frames, match, out):
    lay_heads(out, 0, rms_round(cq[...], gcq[...]))
    lay_heads(out, CTRL_DEV, rms_round(ck[...], gck[...]))
    lay_heads(out, 2 * CTRL_DEV, cv[...])
    spots = jnp.concatenate([match[...]] * 4, axis=1)
    row = lax.broadcasted_iota(jnp.int32, (META, 128), 0)
    meta = jnp.where(row == 0, frames[...], jnp.where(row == 1, spots // 64, spots % 64))
    meta = jnp.where(row < 3, meta, 0).astype(F32).astype(BF16)
    for head in range(HEADS):
        out[head, ROW_M:, :] = meta


def turned(block):
    return block.astype(F32).T.astype(BF16)


def pack_main_kernel(q, k, v, gq, gk, out, q_norm):
    step = 32
    for at in range(0, TOK_DEV, step):
        q_norm[at : at + step, :] = rms_round(q[at : at + step, :], gq[...])
        lay_heads(out, TOK_DEV + at, rms_round(k[at : at + step, :], gk[...]))
    for head in range(HEADS):
        lanes = slice(head * HEAD_DIM, (head + 1) * HEAD_DIM)
        out[head, :TOK_DEV, :] = turned(q_norm[:, lanes])
        out[head, 2 * TOK_DEV :, :] = turned(v[:, lanes])


def ctrl_kernel(places, table, first, hint, ends, notes):
    meta = first[:, ROW_M:, :].astype(F32)
    frames = meta[:, 0, :]
    for f in range(FRAMES):
        ends[f] = jnp.sum(jnp.where(frames <= f + 0.5, 1.0, 0.0)).astype(jnp.int32)
        notes[8 + f : 9 + f, :] = table[pl.ds(places[1 + f], 1), :]
    spots = (meta[:, 1, :] * 64.0 + meta[:, 2, :]).reshape(8, 4, 128)
    source = lax.broadcasted_iota(jnp.int32, (8, 4, 128), 1)
    lane = lax.broadcasted_iota(jnp.int32, (8, 4, 128), 2)
    notes[:8, :] = jnp.sum(jnp.where(lane // CTRL_DEV == source, spots, 0.0), axis=1)
    keys = first[:, CTRL_DEV : 2 * CTRL_DEV, :].reshape(CTRL, HEAD_DIM)
    values = first[:, 2 * CTRL_DEV : ROW_M, :].reshape(CTRL, HEAD_DIM)
    for part in range(4):
        queries = first[part * 8 : part * 8 + 8, :CTRL_DEV, :].reshape(256, HEAD_DIM)
        scores = lax.dot_general(queries, keys, (((1,), (1,)), ((), ())), preferred_element_type=F32)
        top = jnp.max(scores, axis=1, keepdims=True)
        expo = jnp.exp2((scores - top) * SCALE2)
        total = jnp.sum(expo, axis=1, keepdims=True)
        weights = (expo * (1.0 / total)).astype(BF16)
        rows = jnp.dot(weights, values, preferred_element_type=F32).astype(BF16)
        hint[:, part * 256 : part * 256 + 256] = turned(rows)


def main_kernel(
    ends_ref, second, hint, notes_hbm, out, notes, match, gates, v_t, k_mark, acc, sums, top_ref, sem
):
    copy = pltpu.make_async_copy(notes_hbm, notes, sem)
    copy.start()
    ends = [ends_ref[f] for f in range(FRAMES)]

    def end_of(token):
        end = jnp.int32(SEQ)
        for f in reversed(range(FRAMES)):
            end = jnp.where(ends[f] > token, ends[f], end)
        return end

    for block in range(HEADS):
        v_t[:HEAD_DIM, block * 128 : block * 128 + 128] = second[block, 2 * TOK_DEV :, :]
    lane = lax.broadcasted_iota(jnp.int32, (1, 128), 1)
    marks = jnp.full((1, 128), SEQ, jnp.int32)
    for f in range(FRAMES):
        marks = jnp.where(lane == f, ends[f], marks)
    for block in range(HEADS):
        rows = slice(block * TOK_DEV, (block + 1) * TOK_DEV)
        token = lax.broadcasted_iota(jnp.int32, (TOK_DEV, 128), 0) + block * TOK_DEV
        k_mark[rows, :] = jnp.where(token >= marks, 1.0, 0.0).astype(BF16)
    v_t[HEAD_DIM:, :] = jnp.ones((VR - HEAD_DIM, SEQ), BF16)
    copy.wait()
    for g in range(8):
        match[g * 128 : g * 128 + 128, :] = jnp.broadcast_to(notes[g : g + 1, :], (128, 128)).T
        gates[g, :, :] = jnp.broadcast_to(notes[8 + g : 9 + g, :], (128, 128)).T

    def limit_of(base):
        column = lax.broadcasted_iota(jnp.int32, (8, QB), 1) + base
        limit = jnp.full((8, QB), SEQ, jnp.int32)
        for f in reversed(range(FRAMES)):
            limit = jnp.where(ends[f] > column, ends[f], limit)
        return limit[:1, :]

    def queries_of(i):
        per = QB // TOK_DEV
        return jnp.concatenate([second[i * per + n, :TOK_DEV, :] for n in range(per)], axis=1)

    def scores_of(i, j, masked):
        q_t = queries_of(i)
        keys = second[pl.ds(j * (KB // TOK_DEV), KB // TOK_DEV), TOK_DEV : 2 * TOK_DEV, :]
        scores = jnp.dot(keys.reshape(KB, HEAD_DIM), q_t, preferred_element_type=F32)
        return scores

    def visible(limit, j):
        return lax.broadcasted_iota(jnp.int32, (KB, QB), 0) < limit - j * KB

    def values_of(j):
        return v_t[:, pl.ds(pl.multiple_of(j * KB, KB), KB)]

    def finish(i, total):
        base = i * QB
        attn = (total[:HEAD_DIM, :] * (1.0 / total[HEAD_DIM : HEAD_DIM + 1, :])).astype(BF16).astype(F32)
        picks, gate = [], []
        for at in range(0, QB, 128):
            spot = (lax.broadcasted_iota(jnp.int32, (1, 128), 1) + (base + at)).astype(F32)
            picks.append(jnp.where(match[...] == spot, 1.0, 0.0).astype(BF16))
            token = lax.broadcasted_iota(jnp.int32, (HEAD_DIM, 128), 1) + base + at
            level = gates[0]
            for f in range(1, FRAMES):
                level = jnp.where(token >= ends[f - 1], gates[f], level)
            gate.append(level)
        added = jnp.dot(hint[...], jnp.concatenate(picks, axis=1), preferred_element_type=F32)
        mixed = (jnp.concatenate(gate, axis=1) * attn + added).T.astype(BF16)
        rows = QB // TOK_DEV
        out[pl.ds(i * rows, rows), :, :] = mixed.reshape(rows, TOK_DEV, HEAD_DIM)

    def quick_block(i, carry):
        base = i * QB
        q_t = queries_of(i)
        column = lax.broadcasted_iota(jnp.int32, (16, QB), 1) + base
        frame = jnp.zeros((16, QB), jnp.int32)
        for f in range(FRAMES - 1):
            frame = jnp.where(column >= ends[f], f + 1, frame)
        hide = jnp.where(lax.broadcasted_iota(jnp.int32, (16, QB), 0) == frame, -1e30, 0.0)
        q_mark = jnp.concatenate(
            [q_t, hide.astype(BF16), jnp.zeros((HEAD_DIM - 16, QB), BF16)], axis=0
        )

        def run(count):
            finish(jnp.maximum(i - 1, 0), acc)
            held = second[: count * PART // TOK_DEV, TOK_DEV : 2 * TOK_DEV, :]
            keys = jnp.concatenate(
                [held.reshape(count * PART, HEAD_DIM), k_mark[: count * PART, :]], axis=1
            )
            expo = jnp.exp2(jnp.dot(keys, q_mark, preferred_element_type=F32) * SCALE2)
            acc[...] = jnp.dot(
                v_t[:, : count * PART], expo.astype(BF16), preferred_element_type=F32
            )

        parts = (end_of(base + QB - 1) + PART - 1) // PART
        def choose(low, high):
            if low == high:
                run(low)
                return
            middle = (low + high) // 2
            lax.cond(
                parts <= middle, lambda: choose(low, middle), lambda: choose(middle + 1, high)
            )

        choose(1, SEQ // PART)

        sums[pl.ds(i, 1), :] = acc[HEAD_DIM : HEAD_DIM + 1, :]
        return carry

    def full_block(i, carry):
        base = i * QB
        n_all = (end_of(base + QB - 1) + KB - 1) // KB
        limit = limit_of(base)
        acc[...] = jnp.zeros_like(acc)
        top_ref[...] = jnp.full_like(top_ref, -1e30)

        @pl.loop(0, n_all)
        def _(j):
            scores = jnp.where(visible(limit, j), scores_of(i, j, True), -1e30)
            old = top_ref[:1, :]
            new = jnp.maximum(old, jnp.max(scores, axis=0, keepdims=True))
            expo = jnp.exp2((scores - new) * SCALE2).astype(BF16)
            part = jnp.dot(values_of(j), expo, preferred_element_type=F32)
            acc[...] = acc[...] * jnp.exp2((old - new) * SCALE2) + part
            top_ref[...] = jnp.broadcast_to(new, top_ref.shape)

        finish(i, acc)
        return carry

    acc[...] = jnp.ones_like(acc)
    lax.fori_loop(0, SEQ // QB, quick_block, 0)
    finish(SEQ // QB - 1, acc)
    good = (sums[...] > 1.0 / SAFE) & (sums[...] < SAFE)
    count = jnp.sum(jnp.where(good, 1.0, 0.0))

    @pl.when(count < SEQ - 0.5)
    def _():
        lax.fori_loop(0, SEQ // QB, full_block, 0)


def unpack_kernel(rows, out):
    for head in range(HEADS):
        out[:, head * HEAD_DIM : (head + 1) * HEAD_DIM] = rows[head, :, :]


def cost(flops, moved, transcendentals=0):
    return pl.CostEstimate(flops=flops, bytes_accessed=moved, transcendentals=transcendentals)


def shape(*dims, dtype=BF16):
    return jax.ShapeDtypeStruct(dims, dtype)


def run_main(ends, second, hint, notes):
    return pl.pallas_call(
        main_kernel,
        out_shape=shape(HEADS, TOK_DEV, HEAD_DIM),
        in_specs=[pl.BlockSpec(memory_space=pltpu.SMEM)] + [whole()] * 2 + [pl.BlockSpec(memory_space=pltpu.HBM)],
        out_specs=whole(),
        scratch_shapes=[
            pltpu.VMEM((16, 128), F32),
            pltpu.VMEM((CTRL, 128), F32),
            pltpu.VMEM((FRAMES, HEAD_DIM, 128), F32),
            pltpu.VMEM((VR, SEQ), BF16),
            pltpu.VMEM((SEQ, HEAD_DIM), BF16),
            pltpu.VMEM((VR, QB), F32),
            pltpu.VMEM((SEQ // QB, QB), F32),
            pltpu.VMEM((8, QB), F32),
            pltpu.SemaphoreType.DMA,
        ],
        compiler_params=params(),
        cost_estimate=cost(4 * SEQ * SEQ * HEAD_DIM, 5_000_000, SEQ * SEQ),
        name="main_attention",
    )(ends, second, hint, notes)


def exchange(block):
    return lax.all_to_all(block, "seq", split_axis=0, concat_axis=0, tiled=True)


def body(
    query,
    key,
    value,
    gain_query,
    gain_key,
    ctrl_query,
    ctrl_key,
    ctrl_value,
    ctrl_gain_query,
    ctrl_gain_key,
    gate_table,
    levels,
    frame_map,
    control_match,
):
    packed = pl.pallas_call(
        pack_ctrl_kernel,
        out_shape=shape(HEADS, ROWS_C, HEAD_DIM),
        in_specs=[whole()] * 7,
        out_specs=whole(),
        compiler_params=params(56),
        cost_estimate=cost(2_000_000, 2_000_000),
        name="pack_ctrl",
    )(
        ctrl_query[0],
        ctrl_key[0],
        ctrl_value[0],
        ctrl_gain_query[None],
        ctrl_gain_key[None],
        frame_map,
        control_match,
    )
    first = exchange(packed)
    packed_main = pl.pallas_call(
        pack_main_kernel,
        out_shape=shape(HEADS, ROWS, HEAD_DIM),
        in_specs=[whole()] * 5,
        out_specs=whole(),
        scratch_shapes=[pltpu.VMEM((TOK_DEV, WIDTH), BF16)],
        compiler_params=params(),
        cost_estimate=cost(8_000_000, 6_000_000),
        name="pack_main",
    )(query[0], key[0], value[0], gain_query[None], gain_key[None])
    second = exchange(packed_main)
    places = jnp.concatenate([lax.axis_index("seq")[None].astype(jnp.int32), levels[0]])
    hint, ends, notes = pl.pallas_call(
        ctrl_kernel,
        grid_spec=pltpu.PrefetchScalarGridSpec(
            num_scalar_prefetch=1,
            grid=(1,),
            in_specs=[pl.BlockSpec((LEVELS, HEAD_DIM), lambda i, places: (0, places[0])), whole()],
            out_specs=(whole(), pl.BlockSpec(memory_space=pltpu.SMEM), whole()),
        ),
        out_shape=(
            shape(HEAD_DIM, CTRL),
            shape(FRAMES, dtype=jnp.int32),
            shape(16, 128, dtype=F32),
        ),
        compiler_params=params(),
        cost_estimate=cost(4 * CTRL * CTRL * HEAD_DIM, 1_000_000, CTRL * CTRL),
        name="ctrl_attention",
    )(places, gate_table, first)
    groups = lax.axis_size("grp")
    hint = lax.ppermute(hint, "grp", [((i - 1) % groups, i) for i in range(groups)])
    mixed = run_main(ends, second, hint, notes)
    back = exchange(mixed)
    return pl.pallas_call(
        unpack_kernel,
        out_shape=shape(TOK_DEV, WIDTH),
        in_specs=[whole()],
        out_specs=whole(),
        compiler_params=params(),
        cost_estimate=cost(0, 2_000_000),
        name="unpack",
    )(back)[None]


def solution(mesh):
    return jax.shard_map(
        body,
        mesh=mesh,
        in_specs=(
            P("grp", "seq", None),
            P("grp", "seq", None),
            P("grp", "seq", None),
            P(),
            P(),
            P("grp", "seq", None),
            P("grp", "seq", None),
            P("grp", "seq", None),
            P(),
            P(),
            P(),
            P("grp", None),
            P("grp", "seq"),
            P("grp", "seq"),
        ),
        out_specs=P("grp", "seq", None),
        check_vma=False,
    )
```
